32 devices in a mesh: groups: 2 (over y), ctx: 4 (over z), dp: 2 (over x), mp: 2 (over core).
Axes of the slice: x: 2, y: 2, z: 4, core: 2. Of those that a mesh axis runs over, the one named last changes fastest.
Arguments:
- queries: bfloat16 [4, 2048, 1024], P(('groups', 'dp'), 'ctx', 'mp'), parts along dimension 0, may hold values from -6 to 6
- key_vectors: bfloat16 [4, 2048, 1024], P(('groups', 'dp'), 'ctx', 'mp'), parts along dimension 0, may hold values from -1.1953125 to 1.1953125
- value_vectors: bfloat16 [4, 2048, 2048], P(('groups', 'dp'), 'ctx', 'mp'), parts along dimension 0, may hold values from -6 to 6
- log_gates: bfloat16 [4, 2048, 1024], P(('groups', 'dp'), 'ctx', 'mp'), parts along dimension 0, may hold values from -1 to 0
- doc_lengths: int32 [4, 6], P(('groups', 'dp')), parts along dimension 0, may hold values from 1 to 1024, 2048 in all within a row
- cotangent: bfloat16 [4, 2048, 2048], P(('groups', 'dp'), 'ctx'), parts along dimension 0, may hold values from -0.59765625 to 0.59765625
- out_weight: bfloat16 [2048, 2048], P('mp'), may hold values from -0.125 to 0.125
Outputs:
- query_grad: bfloat16 [4, 2048, 1024], P(('groups', 'dp'), 'ctx', 'mp'), parts along dimension 0
- key_grad: bfloat16 [4, 2048, 1024], P(('groups', 'dp'), 'ctx', 'mp'), parts along dimension 0
- value_grad: bfloat16 [4, 2048, 2048], P(('groups', 'dp'), 'ctx', 'mp'), parts along dimension 0
- projection_weight_gradient: float32 [4096, 2048], P(('groups', 'mp'), ('ctx', 'dp')), parts along dimension 0
The draws below stay inside these ranges and needn't reach their ends.
There are 2 independent parts, one for each index of `groups`. The reference program is written for one: setup_inputs(seed, part) draws one part's arguments, and reference() takes and returns one part's arrays. A program takes and returns all parts, laid end to end along the dimension named above; an argument that names none is the same for every part. Nothing has to cross between parts.
Inputs may be any that keep to these rules, and one draw needn't show every extreme that they name: `doc_lengths`: the lengths of one sequence's documents sum to 2048; the longest is 1024.
All inputs are finite; a program needn't handle non-finite values.
Results may differ from the reference program's by a relative error of at most 0.0029.
Values sent between devices are 32-bit elements; how exact they have to be, the bound alone decides.
A program may use at most 128 MiB of HBM per device.

```python
import math
import jax
import jax.numpy as jnp
import numpy as np
from jax import lax

D = 2048
HEADS = 4
KEY = 256
VAL = 512
SPAN = 128
DOCS = 6
TOK_DEV = 512
BATCH = 2
SEQ = 2048


def draw_log_gates(key, part):
    key = jax.random.fold_in(key, 11)
    streams = jax.random.split(key, 7)
    columns = HEADS * KEY
    fast_share = 0.5
    picked = jax.random.uniform(streams[0], (BATCH, 1, columns)) < fast_share
    fast_rate = jnp.exp(jax.random.uniform(streams[1], (BATCH, 1, columns), minval=math.log(1.0 / 50.0), maxval=math.log(1.0 / 30.0)))
    slow_rate = jnp.exp(jax.random.uniform(streams[2], (BATCH, 1, columns), minval=math.log(0.01), maxval=math.log(0.05))) / SEQ
    base_rate = jnp.where(picked, fast_rate, slow_rate)
    device_blocks = SEQ // TOK_DEV
    device_factor = jnp.exp(jax.random.uniform(streams[3], (BATCH, device_blocks, 1, columns), minval=math.log(0.5), maxval=math.log(2.0)))
    jitter = jax.random.uniform(streams[4], (BATCH, device_blocks, TOK_DEV, columns), minval=0.5, maxval=1.5)
    forgetting_speeds = (base_rate[:, :, None, :] * device_factor * jitter).reshape(BATCH, SEQ, columns)
    token_offsets = jax.random.randint(streams[5], (BATCH, 3), 0, SEQ)
    objective_samples = jnp.log(jax.random.uniform(streams[6], (BATCH, 3), minval=0.37, maxval=0.8))
    boundary_flags = jnp.arange(SEQ, dtype=jnp.int32)
    segment_clusters = jnp.sum(jnp.where(boundary_flags[None, :, None] == token_offsets[:, None, :], objective_samples[:, None, :], 0.0), axis=2)
    return jnp.maximum(segment_clusters[:, :, None] - forgetting_speeds, -1.0).astype(jnp.bfloat16)


def strengthened(values, rng, source, target, blocks, factor):
    owner, partner = [(jnp.arange(values.shape[position]) // (values.shape[position] // blocks)).reshape([-1 if axis == position else 1 for axis in range(values.ndim)]) for position in (source, target)]
    chosen = jax.random.permutation(rng, blocks)[partner]
    strong = (owner == chosen) | (owner == (partner + blocks // 2) % blocks)
    return jnp.where(strong, factor * values, values)


def block_levels(rng, dims, cuts, least, top_value):
    def one(position, blocks):
        steps = jax.random.uniform(jax.random.fold_in(jax.random.fold_in(rng, 6), position), (blocks,), jnp.float32, least / len(cuts), top_value / len(cuts))
        return jnp.repeat(jnp.exp(steps), dims[position] // blocks).reshape((-1,) + (1,) * (len(dims) - position - 1))

    gain = one(*cuts[0])
    for cut in cuts[1:]:
        gain = gain * one(*cut)
    return gain


def split_up(number_of, total, limit, lean):
    weights = [(1 << 20) // math.isqrt(standing ** lean) + 1 for standing in range(2, number_of + 1)]
    rest, given = total - limit - (number_of - 1), [1] * (number_of - 1)
    while rest > 0:
        candidates = [i for i in range(number_of - 1) if given[i] < limit]
        mass, left = sum([weights[i] for i in candidates]), rest
        for i in candidates:
            extra = min(limit - given[i], max(1, left * weights[i] // mass), rest)
            given[i] = given[i] + extra
            rest = rest - extra
    return np.array([limit] + given)


def ragged_sizes(key, count, total, limit, skew):
    if count == 2:
        one = jax.random.randint(key, (), max(1, total - limit), min(limit, total - 1) + 1)
        return jnp.stack([one, total - one])
    tallies = jnp.asarray(split_up(count, total, limit, skew), jnp.int32)
    twos = (count - 1) // 2
    donor, sink = tallies[1:1 + 2 * twos:2], tallies[2:2 + 2 * twos:2]
    room = jnp.minimum(donor - 1, limit - sink)
    shifted = jax.random.randint(jax.random.fold_in(key, 1), (twos,), 0, 1 << 20) % (room + 1)
    tallies = tallies.at[1:1 + 2 * twos:2].set(donor - shifted).at[2:2 + 2 * twos:2].set(sink + shifted)
    return tallies[jax.random.permutation(jax.random.fold_in(key, 2), count)]


def scatter_about(key, shape, width, most, pieces=(), kind=jnp.bfloat16):
    drawn = jax.random.normal(key, shape, jnp.float32) * width
    if len(pieces) > 0:
        drawn = block_levels(key, shape, pieces, -0.22, 0.18) * drawn
    return jnp.clip(drawn, min=-most, max=most).astype(kind)


def heavy_noise(rng, dims, width, bound, pieces, heavy, kind=jnp.bfloat16):
    drawn = width * jax.random.normal(rng, dims, jnp.float32)
    if pieces:
        drawn = drawn * block_levels(rng, dims, pieces, -0.22, 0.18)
    return jnp.clip(strengthened(drawn, jax.random.fold_in(rng, 3), *heavy), -bound, bound).astype(kind)


def setup_inputs(seed: int = 0, part: int = 0) -> dict:
    key_list = jax.random.split(jax.random.key(seed), 8)
    part_keys = jax.random.split(jax.random.fold_in(key_list[7], part), 8)
    queries = scatter_about(part_keys[0], (BATCH, SEQ, HEADS * KEY), 1.0, 6.0, ((0, 2), (1, 4), (2, 2)))
    key_vectors = scatter_about(part_keys[1], (BATCH, SEQ, HEADS * KEY), 0.2, 1.1953125, ((0, 2), (1, 4), (2, 2)))
    value_vectors = scatter_about(part_keys[2], (BATCH, SEQ, HEADS * VAL), 1.0, 6.0, ((0, 2), (1, 4), (2, 2)))
    log_gates = draw_log_gates(jax.random.fold_in(jax.random.fold_in(key_list[7], part), 71), part)
    doc_lengths = jax.vmap(lambda own: ragged_sizes(own, DOCS, SEQ, SEQ // 2, 2))(jax.random.split(part_keys[4], BATCH)).reshape((BATCH, DOCS)).astype(jnp.int32)
    cotangent = heavy_noise(part_keys[5], (BATCH, SEQ, D), 0.1, 0.59765625, ((0, 2), (1, 4)), (1, 2, 4, 2.0))
    out_weight = scatter_about(key_list[6], (HEADS * VAL, D), (HEADS * VAL) ** -0.5, 0.125, ((0, 2),))
    return dict(queries=queries, key_vectors=key_vectors, value_vectors=value_vectors, log_gates=log_gates, doc_lengths=doc_lengths, cotangent=cotangent, out_weight=out_weight)


exact_mode = lax.Precision.HIGHEST

def document_of(lengths, positions):
    bounds = jnp.cumsum(lengths)
    return lax.optimization_barrier(jnp.sum((positions[:, None] >= bounds[None, :]).astype(jnp.int32), axis=1))

def to_blocks(matrix, head_count, block_len):
    length, columns = matrix.shape
    shaped = matrix.astype(jnp.float32).reshape(length // block_len, block_len, head_count, columns // head_count)
    return shaped.transpose(0, 2, 1, 3)

def unpack_sections(blocks):
    block_count, head_count, block_len, columns = blocks.shape
    return blocks.transpose(0, 2, 1, 3).reshape(block_count * block_len, head_count * columns)

def block_terms(query_rows, key_rows, value_rows, gate_rows, grad_rows, doc_index, starts):
    cumulative = jnp.cumsum(gate_rows, axis=2)
    growth = jnp.exp(cumulative)
    shrink = jnp.exp(-cumulative)
    final_position = growth[:, :, -1, :]
    block_len = doc_index.shape[1]
    row_ids = lax.broadcasted_iota(jnp.int32, (block_len, block_len), 0)
    col_ids = lax.broadcasted_iota(jnp.int32, (block_len, block_len), 1)
    masking = (row_ids >= col_ids)[None] & (doc_index[:, :, None] == doc_index[:, None, :])
    masking = masking.astype(jnp.float32)[:, None]
    living = (jnp.cumsum(starts, axis=1) == 0).astype(jnp.float32)[:, None, :, None]
    trailing = (doc_index == doc_index[:, -1:]).astype(jnp.float32)[:, None, :, None]
    query_grown = query_rows * growth
    key_shrunk = key_rows * shrink
    key_tail = key_shrunk * final_position[:, :, None, :] * trailing
    query_alive = query_grown * living
    scores = jnp.einsum('nhik,nhjk->nhij', query_grown, key_shrunk, precision=exact_mode) * masking
    mixing = jnp.einsum('nhiv,nhjv->nhij', grad_rows, value_rows, precision=exact_mode) * masking
    decays = final_position * living[:, :, -1, :]
    carried = jnp.einsum('nhjk,nhjv->nhkv', key_tail, value_rows, precision=exact_mode)
    returned = jnp.einsum('nhik,nhiv->nhkv', query_alive, grad_rows, precision=exact_mode)
    return (growth, shrink, final_position, trailing, living, query_grown, key_shrunk, key_tail, query_alive, scores, mixing, decays, carried, returned)

def block_outputs(parts, value_rows, grad_rows, first_states, end_grads):
    growth, shrink, final_position, trailing, living, query_grown, key_shrunk, key_tail, query_alive, scores, mixing = parts[:11]
    outputs = jnp.einsum('nhij,nhjv->nhiv', scores, value_rows, precision=exact_mode)
    outputs = outputs + jnp.einsum('nhik,nhkv->nhiv', query_alive, first_states, precision=exact_mode)
    query_part = jnp.einsum('nhij,nhjk->nhik', mixing, key_shrunk, precision=exact_mode)
    query_part = growth * (query_part + living * jnp.einsum('nhkv,nhiv->nhik', first_states, grad_rows, precision=exact_mode))
    key_part = jnp.einsum('nhij,nhik->nhjk', mixing, query_grown, precision=exact_mode)
    key_part = shrink * (key_part + trailing * final_position[:, :, None, :] * jnp.einsum('nhkv,nhjv->nhjk', end_grads, value_rows, precision=exact_mode))
    value_part = jnp.einsum('nhij,nhiv->nhjv', scores, grad_rows, precision=exact_mode)
    value_part = value_part + jnp.einsum('nhjk,nhkv->nhjv', key_tail, end_grads, precision=exact_mode)
    return (outputs, query_part, key_part, value_part)

def inbound_carry(decays, states, incoming, backward):

    def advance(current, segment_couple):
        return (segment_couple[0][..., None] * current + segment_couple[1], current)
    _, before = lax.scan(advance, incoming, (decays, states), reverse=backward)
    return before

def reference(queries, key_vectors, value_vectors, log_gates, doc_lengths, cotangent, out_weight):
    scaling = KEY ** (-0.5)

    def one_sequence(inputs):
        query_in, key_in, value_in, gate_in, lengths, cotangent_in = inputs
        positions = jnp.arange(SEQ, dtype=jnp.int32)
        doc_index = document_of(lengths, positions)
        before_index = document_of(lengths, positions - 1)
        starts = ((doc_index != before_index) | (positions == 0)).astype(jnp.int32)
        grad_out = jnp.dot(cotangent_in, out_weight.T, preferred_element_type=jnp.float32)
        block_count = SEQ // SPAN
        query_rows = to_blocks(query_in, HEADS, SPAN) * scaling
        key_rows = to_blocks(key_in, HEADS, SPAN)
        value_rows = to_blocks(value_in, HEADS, SPAN)
        gate_rows = to_blocks(gate_in, HEADS, SPAN)
        grad_rows = to_blocks(grad_out, HEADS, SPAN)
        parts = block_terms(query_rows, key_rows, value_rows, gate_rows, grad_rows, doc_index.reshape(block_count, SPAN), starts.reshape(block_count, SPAN))
        decays, carried, returned = (parts[11], parts[12], parts[13])
        zero_state = jnp.zeros((HEADS, KEY, VAL), jnp.float32)
        first_states = inbound_carry(decays, carried, zero_state, False)
        end_grads = inbound_carry(decays, returned, zero_state, True)
        outputs, query_part, key_part, value_part = block_outputs(parts, value_rows, grad_rows, first_states, end_grads)
        attn_out = unpack_sections(outputs).astype(jnp.bfloat16)
        query_grad = (unpack_sections(query_part) * scaling).astype(jnp.bfloat16)
        key_grad = unpack_sections(key_part).astype(jnp.bfloat16)
        value_grad = unpack_sections(value_part).astype(jnp.bfloat16)
        return (attn_out, query_grad, key_grad, value_grad)
    attn_out, query_grad, key_grad, value_grad = lax.map(one_sequence, (queries, key_vectors, value_vectors, log_gates, doc_lengths, cotangent))
    summed = jnp.dot(attn_out.reshape(BATCH * SEQ, HEADS * VAL).T, cotangent.reshape(BATCH * SEQ, D), preferred_element_type=jnp.float32)
    projection_weight_gradient = summed / math.sqrt(BATCH * SEQ)
    return (query_grad, key_grad, value_grad, projection_weight_gradient)
```

```python
import functools
import math

import jax
import jax.numpy as jnp
from jax import lax
from jax.experimental import pallas as pl
from jax.experimental.pallas import tpu as pltpu
from jax.sharding import PartitionSpec as P

KEY = 256
VAL = 512
SPAN = 128
SCALE = KEY ** (-0.5)
VMEM_BYTES = 48 * 1024 * 1024
MESH = pl.DeviceIdType.MESH
F32 = jnp.float32
BF16 = jnp.bfloat16

NN = (((1,), (0,)), ((), ()))
NT = (((1,), (1,)), ((), ()))
TN = (((0,), (0,)), ((), ()))


def dot(a, b, dims):
    return lax.dot_general(a, b, dims, preferred_element_type=F32)


def split(x):
    high = x.astype(BF16)
    return high, (x - high.astype(F32)).astype(BF16)


def whole(x):
    return x, None


def product(a, b, dims):
    out = dot(a[0], b[0], dims)
    if a[1] is not None:
        out = out + dot(a[1], b[0], dims)
    if b[1] is not None:
        out = out + dot(a[0], b[1], dims)
    return out


def bounds_of(lens_ref):
    bounds, total = [], 0
    for d in range(lens_ref.shape[1]):
        total = total + lens_ref[0, d]
        bounds.append(total)
    return bounds


def doc_scalar(bounds, position):
    count = jnp.int32(0)
    for bound in bounds:
        count = count + jnp.where(position >= bound, 1, 0).astype(jnp.int32)
    return count


def doc_array(bounds, first, shape, dim):
    positions = first + lax.broadcasted_iota(jnp.int32, shape, dim)
    count = jnp.zeros(shape, jnp.int32)
    for bound in bounds:
        count = count + jnp.where(positions >= bound, 1, 0)
    return count


def alive_and_trailing(bounds, first, rows, columns):
    docs = doc_array(bounds, first, (rows, columns), 0)
    before = jnp.where(first > 0, doc_scalar(bounds, first - 1), -1)
    last = doc_scalar(bounds, first + rows - 1)
    living = jnp.where(docs == before, 1.0, 0.0).astype(F32)
    trailing = jnp.where(docs == last, 1.0, 0.0).astype(F32)
    return living, trailing


def running_sum(gates):
    rows = gates.shape[0]
    lower = lax.broadcasted_iota(jnp.int32, (rows, rows), 0) >= lax.broadcasted_iota(
        jnp.int32, (rows, rows), 1
    )
    return dot(jnp.where(lower, 1.0, 0.0).astype(BF16), gates, NN)


def states_kernel(lens, q, k, v, gates, cot, weight, grad_o, fwd_o, bwd_o, decay_o):
    tokens = q.shape[0]
    bounds = bounds_of(lens)
    first = lax.axis_index("ctx") * tokens
    grad = dot(cot[...], weight[...], NT)
    grad_o[...] = grad
    cumulative = running_sum(gates[...])
    end = cumulative[tokens - 1 :, :]
    living, trailing = alive_and_trailing(bounds, first, tokens, KEY)
    tail = k[...].astype(F32) * jnp.exp(end - cumulative) * trailing
    alive = q[...].astype(F32) * SCALE * jnp.exp(cumulative) * living
    fwd_o[...] = product(whole(v[...]), split(tail), TN)
    bwd_o[...] = product(split(grad), split(alive), TN)
    decay_o[...] = (jnp.exp(end) * living[tokens - 1 :, :])[None]


def chain_kernel(n, pieces, fwd, bwd, decay, fwd_in, bwd_in, f_send, b_send, f_recv, b_recv, sems):
    me = lax.axis_index("ctx")
    rows = fwd.shape[0] // pieces
    per_head = pieces // decay.shape[0]
    has_left, has_right = me > 0, me < n - 1
    barrier = pltpu.get_barrier_semaphore()

    @pl.when(has_left)
    def _():
        pl.semaphore_signal(barrier, inc=1, device_id={"ctx": me - 1}, device_id_type=MESH)

    @pl.when(has_right)
    def _():
        pl.semaphore_signal(barrier, inc=1, device_id={"ctx": me + 1}, device_id_type=MESH)

    pl.semaphore_wait(barrier, has_left.astype(jnp.int32) + has_right.astype(jnp.int32))

    def copy_of(c, send, recv, base, to):
        at = pl.ds(pl.multiple_of(c * rows, rows), rows)
        return pltpu.make_async_remote_copy(
            src_ref=send.at[at],
            dst_ref=recv.at[at],
            send_sem=sems.at[base, c],
            recv_sem=sems.at[base + 1, c],
            device_id={"ctx": to},
            device_id_type=MESH,
        )

    def one(c, own, send, recv, result, base, has_source, has_target, to):
        at = pl.ds(pl.multiple_of(c * rows, rows), rows)

        @pl.when(has_source)
        def _():
            copy_of(c, send, recv, base, to).wait_recv()
            result[at, :] = recv[at, :]

        @pl.when(jnp.logical_not(has_source))
        def _():
            result[at, :] = jnp.zeros((rows, KEY), F32)

        @pl.when(has_target)
        def _():
            send[at, :] = decay[c // per_head] * result[at, :] + own[at, :]
            copy_of(c, send, recv, base, to).start()

    right = jnp.minimum(me + 1, n - 1)
    left = jnp.maximum(me - 1, 0)

    def slot(s, carry):
        up = s - me
        down = s - (n - 1 - me)

        @pl.when((up >= 0) & (up < pieces))
        def _():
            one(up, fwd, f_send, f_recv, fwd_in, 0, has_left, has_right, right)

        @pl.when((down >= 0) & (down < pieces))
        def _():
            one(down, bwd, b_send, b_recv, bwd_in, 2, has_right, has_left, left)

        return carry

    lax.fori_loop(0, pieces + n - 1, slot, 0)

    def finish(c, carry):
        @pl.when(has_right)
        def _():
            copy_of(c, f_send, f_recv, 0, right).wait_send()

        @pl.when(has_left)
        def _():
            copy_of(c, b_send, b_recv, 2, left).wait_send()

        return carry

    lax.fori_loop(0, pieces, finish, 0)


def outputs_kernel(lens, q, k, v, gates, grad, fwd, bwd, *rest):
    q_o, k_o, v_o, attn_o, scores_s, mixing_s, grown_s, cum_s = rest[-8:]
    tokens = q.shape[0]
    blocks = tokens // SPAN
    bounds = bounds_of(lens)
    device_first = lax.axis_index("ctx") * tokens
    state = fwd[...]
    for n in range(blocks):
        at = slice(n * SPAN, (n + 1) * SPAN)
        first = device_first + n * SPAN
        cumulative = running_sum(gates[at, :])
        cum_s[at, :] = cumulative
        growth = jnp.exp(cumulative)
        shrink = jnp.exp(-cumulative)
        end = cumulative[SPAN - 1 :, :]
        living, trailing = alive_and_trailing(bounds, first, SPAN, KEY)
        rows = lax.broadcasted_iota(jnp.int32, (SPAN, SPAN), 0)
        columns = lax.broadcasted_iota(jnp.int32, (SPAN, SPAN), 1)
        same = doc_array(bounds, first, (SPAN, SPAN), 0) == doc_array(bounds, first, (SPAN, SPAN), 1)
        mask = jnp.where((rows >= columns) & same, 1.0, 0.0).astype(F32)
        value = whole(v[at, :])
        key = k[at, :].astype(F32)
        grown = q[at, :].astype(F32) * SCALE * growth
        grown_s[at, :] = grown
        shrunk = key * shrink
        grown_p, shrunk_p, grad_p = split(grown), split(shrunk), split(grad[at, :])
        scores = product(grown_p, shrunk_p, NT) * mask
        mixing = product(grad_p, value, NT) * mask
        scores_s[at, :] = scores
        mixing_s[at, :] = mixing
        state_p = split(state)
        alive = split(grown * living)
        out = product(split(scores), value, NN) + product(alive, state_p, NT)
        attn_o[at, :] = out.astype(BF16).astype(F32)
        dq = product(split(mixing), shrunk_p, NN) + living * product(grad_p, state_p, NN)
        q_o[at, :] = (growth * dq * SCALE).astype(BF16)
        if n < blocks - 1:
            tail = split(key * jnp.exp(end - cumulative) * trailing)
            decay = jnp.exp(end) * living[SPAN - 1 :, :]
            state = decay * state + product(value, tail, TN)
    state = bwd[...]
    for n in reversed(range(blocks)):
        at = slice(n * SPAN, (n + 1) * SPAN)
        first = device_first + n * SPAN
        cumulative = cum_s[at, :]
        shrink = jnp.exp(-cumulative)
        end = cumulative[SPAN - 1 :, :]
        living, trailing = alive_and_trailing(bounds, first, SPAN, KEY)
        value = whole(v[at, :])
        grad_p = split(grad[at, :])
        grown = grown_s[at, :]
        from_end = jnp.exp(end - cumulative) * trailing
        tail = split(k[at, :].astype(F32) * from_end)
        state_p = split(state)
        dk = shrink * product(split(mixing_s[at, :]), split(grown), TN)
        dk = dk + from_end * product(value, state_p, NN)
        k_o[at, :] = dk.astype(BF16)
        dv = product(split(scores_s[at, :]), grad_p, TN) + product(tail, state_p, NT)
        v_o[at, :] = dv.astype(BF16)
        if n > 0:
            decay = jnp.exp(end) * living[SPAN - 1 :, :]
            state = decay * state + product(grad_p, split(grown * living), TN)


def weight_kernel(peers, norm, *refs):
    out = refs[-1]
    total = None
    for p in range(peers):
        term = dot(refs[p][...].astype(BF16), refs[peers + p][0].astype(BF16), TN)
        total = term if total is None else total + term
    out[...] = (total * norm)[None]


def params(**more):
    return pltpu.CompilerParams(vmem_limit_bytes=VMEM_BYTES, **more)


def per_device(queries, key_vectors, value_vectors, log_gates, doc_lengths, cotangent, out_weight):
    q, k, v, gates, cot = (x[0] for x in (queries, key_vectors, value_vectors, log_gates, cotangent))
    tokens, width = cot.shape
    heads = out_weight.shape[0] // VAL
    n, peers = lax.axis_size("ctx"), lax.axis_size("dp")
    dp = lax.axis_index("dp")
    columns = width // (n * peers)
    smem = pl.BlockSpec(memory_space=pltpu.SMEM)

    parted = cot.reshape(tokens, n, peers, columns)

    def part_for(p):
        return lax.dynamic_index_in_dim(parted, p, axis=2, keepdims=False).transpose(1, 0, 2)

    def shift(x, s):
        return lax.ppermute(x, "dp", [(i, (i + s) % peers) for i in range(peers)])

    cots = [part_for(dp)]
    for s in range(1, peers):
        cots.append(shift(part_for(lax.rem(dp + s, peers)).astype(F32), s))

    def head_block(rows, cols):
        return pl.BlockSpec((rows, cols), lambda h: (0, h))

    def head_rows(rows, cols):
        return pl.BlockSpec((rows, cols), lambda h: (h, 0))

    grad, fwd, bwd, decay = pl.pallas_call(
        states_kernel,
        grid=(heads,),
        in_specs=[
            smem,
            head_block(tokens, KEY),
            head_block(tokens, KEY),
            head_block(tokens, VAL),
            head_block(tokens, KEY),
            pl.BlockSpec((tokens, width), lambda h: (0, 0)),
            head_rows(VAL, width),
        ],
        out_specs=[
            head_block(tokens, VAL),
            head_rows(VAL, KEY),
            head_rows(VAL, KEY),
            pl.BlockSpec((1, 1, KEY), lambda h: (h, 0, 0)),
        ],
        out_shape=[
            jax.ShapeDtypeStruct((tokens, heads * VAL), F32),
            jax.ShapeDtypeStruct((heads * VAL, KEY), F32),
            jax.ShapeDtypeStruct((heads * VAL, KEY), F32),
            jax.ShapeDtypeStruct((heads, 1, KEY), F32),
        ],
        compiler_params=params(),
        cost_estimate=pl.CostEstimate(flops=6 * 10**9, bytes_accessed=14 << 20, transcendentals=0),
        name="states",
    )(doc_lengths, q, k, v, gates, cot, out_weight)

    pieces = 8 * heads
    vmem = pl.BlockSpec(memory_space=pltpu.VMEM)
    state_shape = (heads * VAL, KEY)
    fwd_in, bwd_in = pl.pallas_call(
        functools.partial(chain_kernel, n, pieces),
        in_specs=[vmem] * 3,
        out_specs=[vmem] * 2,
        out_shape=[jax.ShapeDtypeStruct(state_shape, F32)] * 2,
        scratch_shapes=[pltpu.VMEM(state_shape, F32)] * 4 + [pltpu.SemaphoreType.DMA((4, pieces))],
        compiler_params=params(collective_id=0, has_side_effects=True),
        cost_estimate=pl.CostEstimate(flops=10**6, bytes_accessed=64 << 20, transcendentals=0),
        name="chain",
    )(fwd, bwd, decay)

    grads = []
    attn = []
    for h in range(heads):
        def cols(c, h=h):
            return pl.BlockSpec((tokens, c), lambda i: (0, h))

        def state_rows(h=h):
            return pl.BlockSpec((VAL, KEY), lambda i: (h, 0))

        results = pl.pallas_call(
            outputs_kernel,
            grid=(1,),
            in_specs=[smem, cols(KEY), cols(KEY), cols(VAL), cols(KEY), cols(VAL)]
            + [state_rows()] * 2
            + [pl.BlockSpec(memory_space=pl.ANY)] * len(grads),
            out_specs=[
                cols(KEY),
                cols(KEY),
                cols(VAL),
                pl.BlockSpec((tokens, VAL), lambda i: (0, 0)),
            ],
            out_shape=[
                jax.ShapeDtypeStruct((tokens, heads * KEY), BF16),
                jax.ShapeDtypeStruct((tokens, heads * KEY), BF16),
                jax.ShapeDtypeStruct((tokens, heads * VAL), BF16),
                jax.ShapeDtypeStruct((tokens, VAL), F32),
            ],
            scratch_shapes=[
                pltpu.VMEM((tokens, SPAN), F32),
                pltpu.VMEM((tokens, SPAN), F32),
                pltpu.VMEM((tokens, KEY), F32),
                pltpu.VMEM((tokens, KEY), F32),
            ],
            input_output_aliases={8 + i: i for i in range(len(grads))},
            compiler_params=params(),
            cost_estimate=pl.CostEstimate(flops=3 * 10**9, bytes_accessed=8 << 20, transcendentals=0),
            name="outputs",
        )(doc_lengths, q, k, v, gates, grad, fwd_in, bwd_in, *grads)
        grads = list(results[:3])
        attn.append(results[3])

    norm = 1.0 / math.sqrt(peers * n * tokens)
    sums = []
    for h in range(heads):
        everyone = [attn[h]] + [shift(attn[h], s) for s in range(1, peers)]
        partial = pl.pallas_call(
            functools.partial(weight_kernel, peers, norm),
            grid=(n,),
            in_specs=[pl.BlockSpec((tokens, VAL), lambda c: (0, 0))] * peers
            + [pl.BlockSpec((1, tokens, columns), lambda c: (c, 0, 0))] * peers,
            out_specs=pl.BlockSpec((1, VAL, columns), lambda c: (c, 0, 0)),
            out_shape=jax.ShapeDtypeStruct((n, VAL, columns), F32),
            compiler_params=params(),
            cost_estimate=pl.CostEstimate(flops=2 * 10**9, bytes_accessed=8 << 20, transcendentals=0),
            name="weight",
        )(*everyone, *cots)
        sums.append(lax.psum_scatter(partial, "ctx", scatter_dimension=0, tiled=True)[0])
    weight_grad = jnp.concatenate(sums, axis=0)
    return (grads[0][None], grads[1][None], grads[2][None], weight_grad)


def solution(mesh):
    batch = ("groups", "dp")
    return jax.shard_map(
        per_device,
        mesh=mesh,
        in_specs=(
            P(batch, "ctx", "mp"),
            P(batch, "ctx", "mp"),
            P(batch, "ctx", "mp"),
            P(batch, "ctx", "mp"),
            P(batch, None),
            P(batch, "ctx", None),
            P("mp", None),
        ),
        out_specs=(
            P(batch, "ctx", "mp"),
            P(batch, "ctx", "mp"),
            P(batch, "ctx", "mp"),
            P(("groups", "mp"), ("ctx", "dp")),
        ),
        check_vma=False,
    )
```

```python
import functools
import math

import jax
import jax.numpy as jnp
from jax import lax
from jax.experimental import pallas as pl
from jax.experimental.pallas import tpu as pltpu
from jax.sharding import PartitionSpec as P

KEY = 256
VAL = 512
SPAN = 128
SKEW = 3
PIECE = 256
SCALE = KEY ** (-0.5)
VMEM_BYTES = 48 * 1024 * 1024
MESH = pl.DeviceIdType.MESH
F32 = jnp.float32
BF16 = jnp.bfloat16

NN = (((1,), (0,)), ((), ()))
NT = (((1,), (1,)), ((), ()))
TN = (((0,), (0,)), ((), ()))


def dot(a, b, dims):
    return lax.dot_general(a, b, dims, preferred_element_type=F32)


def split(x):
    high = x.astype(BF16)
    return high, (x - high.astype(F32)).astype(BF16)


def whole(x):
    return x, None


def product(a, b, dims):
    out = dot(a[0], b[0], dims)
    if a[1] is not None:
        out = out + dot(a[1], b[0], dims)
    if b[1] is not None:
        out = out + dot(a[0], b[1], dims)
    return out


def bounds_of(lens_ref):
    bounds, total = [], 0
    for d in range(lens_ref.shape[1]):
        total = total + lens_ref[0, d]
        bounds.append(total)
    return bounds


def doc_scalar(bounds, position):
    count = jnp.int32(0)
    for bound in bounds:
        count = count + jnp.where(position >= bound, 1, 0).astype(jnp.int32)
    return count


def doc_array(bounds, first, shape, dim):
    positions = first + lax.broadcasted_iota(jnp.int32, shape, dim)
    count = jnp.zeros(shape, jnp.int32)
    for bound in bounds:
        count = count + jnp.where(positions >= bound, 1, 0)
    return count


def alive_and_trailing(bounds, first, rows, columns):
    docs = doc_array(bounds, first, (rows, columns), 0)
    before = jnp.where(first > 0, doc_scalar(bounds, first - 1), -1)
    last = doc_scalar(bounds, first + rows - 1)
    living = jnp.where(docs == before, 1.0, 0.0).astype(F32)
    trailing = jnp.where(docs == last, 1.0, 0.0).astype(F32)
    return living, trailing


def running_sum(gates):
    rows = gates.shape[0]
    lower = lax.broadcasted_iota(jnp.int32, (rows, rows), 0) >= lax.broadcasted_iota(
        jnp.int32, (rows, rows), 1
    )
    return dot(jnp.where(lower, 1.0, 0.0).astype(BF16), gates, NN)


def states_kernel(lens, q, k, v, gates, cot, weight, grad_o, fwd_o, bwd_o, decay_o):
    tokens = q.shape[0]
    bounds = bounds_of(lens)
    first = lax.axis_index("ctx") * tokens
    grad = dot(cot[...], weight[...], NT)
    grad_o[...] = grad
    cumulative = running_sum(gates[...])
    end = cumulative[tokens - 1 :, :]
    living, trailing = alive_and_trailing(bounds, first, tokens, KEY)
    tail = k[...].astype(F32) * jnp.exp(end - cumulative) * trailing
    alive = q[...].astype(F32) * SCALE * jnp.exp(cumulative) * living
    fwd_o[...] = product(whole(v[...]), split(tail), TN)
    bwd_o[...] = product(split(grad), split(alive), TN)
    decay_o[...] = (jnp.exp(end) * living[tokens - 1 :, :])[None]


def chain_kernel(n, pieces, fwd, bwd, decay, fwd_in, bwd_in, f_send, b_send, f_recv, b_recv, sems):
    me = lax.axis_index("ctx")
    rows = fwd.shape[0] // pieces
    per_head = pieces // decay.shape[0]
    has_left, has_right = me > 0, me < n - 1
    barrier = pltpu.get_barrier_semaphore()

    @pl.when(has_left)
    def _():
        pl.semaphore_signal(barrier, inc=1, device_id={"ctx": me - 1}, device_id_type=MESH)

    @pl.when(has_right)
    def _():
        pl.semaphore_signal(barrier, inc=1, device_id={"ctx": me + 1}, device_id_type=MESH)

    pl.semaphore_wait(barrier, has_left.astype(jnp.int32) + has_right.astype(jnp.int32))

    def copy_of(c, send, recv, base, to):
        at = pl.ds(pl.multiple_of(c * rows, rows), rows)
        return pltpu.make_async_remote_copy(
            src_ref=send.at[at],
            dst_ref=recv.at[at],
            send_sem=sems.at[base, c],
            recv_sem=sems.at[base + 1, c],
            device_id={"ctx": to},
            device_id_type=MESH,
        )

    def one(c, own, send, recv, result, base, has_source, has_target, to):
        at = pl.ds(pl.multiple_of(c * rows, rows), rows)

        @pl.when(has_source)
        def _():
            copy_of(c, send, recv, base, to).wait_recv()
            result[at, :] = recv[at, :]

        @pl.when(jnp.logical_not(has_source))
        def _():
            result[at, :] = jnp.zeros((rows, KEY), F32)

        @pl.when(has_target)
        def _():
            send[at, :] = decay[c // per_head] * result[at, :] + own[at, :]
            copy_of(c, send, recv, base, to).start()

    right = jnp.minimum(me + 1, n - 1)
    left = jnp.maximum(me - 1, 0)

    def slot(s, carry):
        up = s - SKEW * me
        down = s - SKEW * (n - 1 - me)

        @pl.when((up >= 0) & (up < pieces))
        def _():
            one(up, fwd, f_send, f_recv, fwd_in, 0, has_left, has_right, right)

        @pl.when((down >= 0) & (down < pieces))
        def _():
            one(down, bwd, b_send, b_recv, bwd_in, 2, has_right, has_left, left)

        return carry

    lax.fori_loop(0, pieces + SKEW * (n - 1), slot, 0)

    def finish(c, carry):
        @pl.when(has_right)
        def _():
            copy_of(c, f_send, f_recv, 0, right).wait_send()

        @pl.when(has_left)
        def _():
            copy_of(c, b_send, b_recv, 2, left).wait_send()

        return carry

    lax.fori_loop(0, pieces, finish, 0)


def outputs_kernel(
    lens, q, k, v, gates, grad, fwd, bwd, q_o, k_o, v_o, attn_o, scores_s, mixing_s, grown_s, cum_s
):
    tokens = q.shape[0]
    blocks = tokens // SPAN
    bounds = bounds_of(lens)
    device_first = lax.axis_index("ctx") * tokens
    state = fwd[...]
    for n in range(blocks):
        at = slice(n * SPAN, (n + 1) * SPAN)
        first = device_first + n * SPAN
        cumulative = running_sum(gates[at, :])
        cum_s[at, :] = cumulative
        growth = jnp.exp(cumulative)
        shrink = jnp.exp(-cumulative)
        end = cumulative[SPAN - 1 :, :]
        living, trailing = alive_and_trailing(bounds, first, SPAN, KEY)
        rows = lax.broadcasted_iota(jnp.int32, (SPAN, SPAN), 0)
        columns = lax.broadcasted_iota(jnp.int32, (SPAN, SPAN), 1)
        same = doc_array(bounds, first, (SPAN, SPAN), 0) == doc_array(bounds, first, (SPAN, SPAN), 1)
        mask = jnp.where((rows >= columns) & same, 1.0, 0.0).astype(F32)
        value = whole(v[at, :])
        key = k[at, :].astype(F32)
        grown = q[at, :].astype(F32) * SCALE * growth
        grown_s[at, :] = grown
        shrunk = key * shrink
        grown_p, shrunk_p, grad_p = split(grown), split(shrunk), split(grad[at, :])
        scores = product(grown_p, shrunk_p, NT) * mask
        mixing = product(grad_p, value, NT) * mask
        scores_s[at, :] = scores
        mixing_s[at, :] = mixing
        state_p = split(state)
        alive = split(grown * living)
        out = product(split(scores), value, NN) + product(alive, state_p, NT)
        out = out.astype(BF16).astype(F32)
        for p in range(VAL // PIECE):
            attn_o[p, at, :] = out[:, p * PIECE : (p + 1) * PIECE]
        dq = product(split(mixing), shrunk_p, NN) + living * product(grad_p, state_p, NN)
        q_o[at, :] = (growth * dq * SCALE).astype(BF16)
        if n < blocks - 1:
            tail = split(key * jnp.exp(end - cumulative) * trailing)
            decay = jnp.exp(end) * living[SPAN - 1 :, :]
            state = decay * state + product(value, tail, TN)
    state = bwd[...]
    for n in reversed(range(blocks)):
        at = slice(n * SPAN, (n + 1) * SPAN)
        first = device_first + n * SPAN
        cumulative = cum_s[at, :]
        shrink = jnp.exp(-cumulative)
        end = cumulative[SPAN - 1 :, :]
        living, trailing = alive_and_trailing(bounds, first, SPAN, KEY)
        value = whole(v[at, :])
        grad_p = split(grad[at, :])
        grown = grown_s[at, :]
        from_end = jnp.exp(end - cumulative) * trailing
        tail = split(k[at, :].astype(F32) * from_end)
        state_p = split(state)
        dk = shrink * product(split(mixing_s[at, :]), split(grown), TN)
        dk = dk + from_end * product(value, state_p, NN)
        k_o[at, :] = dk.astype(BF16)
        dv = product(split(scores_s[at, :]), grad_p, TN) + product(tail, state_p, NT)
        v_o[at, :] = dv.astype(BF16)
        if n > 0:
            decay = jnp.exp(end) * living[SPAN - 1 :, :]
            state = decay * state + product(grad_p, split(grown * living), TN)


def weight_kernel(n, peers, norm, *refs):
    attn, cots, out = refs[0], refs[1 : 1 + peers], refs[1 + peers]
    attn_in, part, ring_in, attn_send, attn_recv, ring_send, ring_recv = refs[2 + peers :]
    pieces = attn.shape[0]
    half = PIECE // 2
    me, dp = lax.axis_index("ctx"), lax.axis_index("dp")
    right, left = lax.rem(me + 1, n), lax.rem(me + n - 1, n)
    others = [lax.rem(dp + s, peers) for s in range(1, peers)]

    barrier = pltpu.get_barrier_semaphore()
    for other in others:
        pl.semaphore_signal(barrier, inc=1, device_id={"dp": other}, device_id_type=MESH)
    for near in (left, right):
        pl.semaphore_signal(barrier, inc=1, device_id={"ctx": near}, device_id_type=MESH)
    pl.semaphore_wait(barrier, len(others) + 2)

    def attn_copy(p, j):
        return pltpu.make_async_remote_copy(
            src_ref=attn.at[j],
            dst_ref=attn_in.at[p, j],
            send_sem=attn_send.at[p, j],
            recv_sem=attn_recv.at[p, j],
            device_id={"dp": others[p]},
            device_id_type=MESH,
        )

    def chunk_at(way, step):
        if way == 0:
            return lax.rem(me - 1 - step + 2 * n, n)
        return lax.rem(me + 1 + step, n)

    def ring_copy(j, way, step):
        return pltpu.make_async_remote_copy(
            src_ref=part.at[j, chunk_at(way, step), pl.ds(way * half, half)],
            dst_ref=ring_in.at[j, way, step],
            send_sem=ring_send.at[j, way, step],
            recv_sem=ring_recv.at[j, way, step],
            device_id={"ctx": right if way == 0 else left},
            device_id_type=MESH,
        )

    for j in range(pieces):
        for p in range(peers - 1):
            attn_copy(p, j).start()

    def multiply(j):
        for p in range(peers - 1):
            attn_copy(p, j).wait_recv()
        rows = [attn[j].astype(BF16)] + [attn_in[p, j].astype(BF16) for p in range(peers - 1)]
        for c in range(n):
            total = dot(rows[0], cots[0][c], TN)
            for p in range(1, peers):
                total = total + dot(rows[p], cots[p][c].astype(BF16), TN)
            part[j, c] = total
        for way in range(2):
            ring_copy(j, way, 0).start()

    def pass_on(j, step):
        for way in range(2):
            ring_copy(j, way, step - 1).wait_recv()
            c = chunk_at(way, step)
            rows = pl.ds(way * half, half)
            total = part[j, c, rows, :] + ring_in[j, way, step - 1]
            if step < n - 1:
                part[j, c, rows, :] = total
                ring_copy(j, way, step).start()
            else:
                out[pl.ds(j * PIECE + way * half, half), :] = total * norm

    for t in range(pieces + n - 1):
        if t < pieces:
            multiply(t)
        for j in range(pieces):
            if 1 <= t - j <= n - 1:
                pass_on(j, t - j)

    for j in range(pieces):
        for p in range(peers - 1):
            attn_copy(p, j).wait_send()
        for way in range(2):
            for step in range(n - 1):
                ring_copy(j, way, step).wait_send()


def params(**more):
    return pltpu.CompilerParams(vmem_limit_bytes=VMEM_BYTES, **more)


def per_device(queries, key_vectors, value_vectors, log_gates, doc_lengths, cotangent, out_weight):
    q, k, v, gates, cot = (x[0] for x in (queries, key_vectors, value_vectors, log_gates, cotangent))
    tokens, width = cot.shape
    heads = out_weight.shape[0] // VAL
    n, peers = lax.axis_size("ctx"), lax.axis_size("dp")
    dp = lax.axis_index("dp")
    columns = width // (n * peers)
    smem = pl.BlockSpec(memory_space=pltpu.SMEM)

    parted = cot.reshape(tokens, n, peers, columns)

    def part_for(p):
        return lax.dynamic_index_in_dim(parted, p, axis=2, keepdims=False).transpose(1, 0, 2)

    def shift(x, s):
        return lax.ppermute(x, "dp", [(i, (i + s) % peers) for i in range(peers)])

    cots = [part_for(dp)]
    for s in range(1, peers):
        cots.append(shift(part_for(lax.rem(dp + s, peers)).astype(F32), s))

    def head_block(rows, cols):
        return pl.BlockSpec((rows, cols), lambda h: (0, h))

    def head_rows(rows, cols):
        return pl.BlockSpec((rows, cols), lambda h: (h, 0))

    grad, fwd, bwd, decay = pl.pallas_call(
        states_kernel,
        grid=(heads,),
        in_specs=[
            smem,
            head_block(tokens, KEY),
            head_block(tokens, KEY),
            head_block(tokens, VAL),
            head_block(tokens, KEY),
            pl.BlockSpec((tokens, width), lambda h: (0, 0)),
            head_rows(VAL, width),
        ],
        out_specs=[
            head_block(tokens, VAL),
            head_rows(VAL, KEY),
            head_rows(VAL, KEY),
            pl.BlockSpec((1, 1, KEY), lambda h: (h, 0, 0)),
        ],
        out_shape=[
            jax.ShapeDtypeStruct((tokens, heads * VAL), F32),
            jax.ShapeDtypeStruct((heads * VAL, KEY), F32),
            jax.ShapeDtypeStruct((heads * VAL, KEY), F32),
            jax.ShapeDtypeStruct((heads, 1, KEY), F32),
        ],
        compiler_params=params(),
        cost_estimate=pl.CostEstimate(flops=6 * 10**9, bytes_accessed=14 << 20, transcendentals=0),
        name="states",
    )(doc_lengths, q, k, v, gates, cot, out_weight)

    pieces = 8 * heads
    vmem = pl.BlockSpec(memory_space=pltpu.VMEM)
    state_shape = (heads * VAL, KEY)
    fwd_in, bwd_in = pl.pallas_call(
        functools.partial(chain_kernel, n, pieces),
        in_specs=[vmem] * 3,
        out_specs=[vmem] * 2,
        out_shape=[jax.ShapeDtypeStruct(state_shape, F32)] * 2,
        scratch_shapes=[pltpu.VMEM(state_shape, F32)] * 4 + [pltpu.SemaphoreType.DMA((4, pieces))],
        compiler_params=params(collective_id=0, has_side_effects=True),
        cost_estimate=pl.CostEstimate(flops=10**6, bytes_accessed=64 << 20, transcendentals=0),
        name="chain",
    )(fwd, bwd, decay)

    def state_rows():
        return pl.BlockSpec((VAL, KEY), lambda h: (h, 0))

    per_head = VAL // PIECE
    query_grad, key_grad, value_grad, attn = pl.pallas_call(
        outputs_kernel,
        grid=(heads,),
        in_specs=[smem]
        + [head_block(tokens, c) for c in (KEY, KEY, VAL, KEY, VAL)]
        + [state_rows()] * 2,
        out_specs=[
            head_block(tokens, KEY),
            head_block(tokens, KEY),
            head_block(tokens, VAL),
            pl.BlockSpec((per_head, tokens, PIECE), lambda h: (h, 0, 0)),
        ],
        out_shape=[
            jax.ShapeDtypeStruct((tokens, heads * KEY), BF16),
            jax.ShapeDtypeStruct((tokens, heads * KEY), BF16),
            jax.ShapeDtypeStruct((tokens, heads * VAL), BF16),
            jax.ShapeDtypeStruct((heads * per_head, tokens, PIECE), F32),
        ],
        scratch_shapes=[
            pltpu.VMEM((tokens, SPAN), F32),
            pltpu.VMEM((tokens, SPAN), F32),
            pltpu.VMEM((tokens, KEY), F32),
            pltpu.VMEM((tokens, KEY), F32),
        ],
        compiler_params=params(),
        cost_estimate=pl.CostEstimate(flops=6 * 10**9, bytes_accessed=16 << 20, transcendentals=0),
        name="outputs",
    )(doc_lengths, q, k, v, gates, grad, fwd_in, bwd_in)

    norm = 1.0 / math.sqrt(peers * n * tokens)
    parts = heads * per_head
    dma = pltpu.SemaphoreType.DMA
    weight_grad = pl.pallas_call(
        functools.partial(weight_kernel, n, peers, norm),
        in_specs=[vmem] * (1 + peers),
        out_specs=vmem,
        out_shape=jax.ShapeDtypeStruct((heads * VAL, columns), F32),
        scratch_shapes=[
            pltpu.VMEM((peers - 1, parts, tokens, PIECE), F32),
            pltpu.VMEM((parts, n, PIECE, columns), F32),
            pltpu.VMEM((parts, 2, n - 1, PIECE // 2, columns), F32),
            dma((peers - 1, parts)),
            dma((peers - 1, parts)),
            dma((parts, 2, n - 1)),
            dma((parts, 2, n - 1)),
        ],
        compiler_params=params(collective_id=1, has_side_effects=True),
        cost_estimate=pl.CostEstimate(flops=4 * 10**9, bytes_accessed=64 << 20, transcendentals=0),
        name="weight",
    )(attn, *cots)
    return (query_grad[None], key_grad[None], value_grad[None], weight_grad)


def solution(mesh):
    batch = ("groups", "dp")
    return jax.shard_map(
        per_device,
        mesh=mesh,
        in_specs=(
            P(batch, "ctx", "mp"),
            P(batch, "ctx", "mp"),
            P(batch, "ctx", "mp"),
            P(batch, "ctx", "mp"),
            P(batch, None),
            P(batch, "ctx", None),
            P("mp", None),
        ),
        out_specs=(
            P(batch, "ctx", "mp"),
            P(batch, "ctx", "mp"),
            P(batch, "ctx", "mp"),
            P(("groups", "mp"), ("ctx", "dp")),
        ),
        check_vma=False,
    )
```

```python
import functools
import math

import jax
import jax.numpy as jnp
from jax import lax
from jax.experimental import pallas as pl
from jax.experimental.pallas import tpu as pltpu
from jax.sharding import PartitionSpec as P

KEY = 256
VAL = 512
SPAN = 128
SKEW = 3
PIECE = 256
SCALE = KEY ** (-0.5)
VMEM_BYTES = 60 * 1024 * 1024
MESH = pl.DeviceIdType.MESH
F32 = jnp.float32
BF16 = jnp.bfloat16

NN = (((1,), (0,)), ((), ()))
NT = (((1,), (1,)), ((), ()))
TN = (((0,), (0,)), ((), ()))


def dot(a, b, dims):
    return lax.dot_general(a, b, dims, preferred_element_type=F32)


def split(x):
    high = x.astype(BF16)
    return high, (x - high.astype(F32)).astype(BF16)


def whole(x):
    return x, None


def product(a, b, dims):
    out = dot(a[0], b[0], dims)
    if a[1] is not None:
        out = out + dot(a[1], b[0], dims)
    if b[1] is not None:
        out = out + dot(a[0], b[1], dims)
    return out


def bounds_of(lens_ref):
    bounds, total = [], 0
    for d in range(lens_ref.shape[1]):
        total = total + lens_ref[0, d]
        bounds.append(total)
    return bounds


def doc_scalar(bounds, position):
    count = jnp.int32(0)
    for bound in bounds:
        count = count + jnp.where(position >= bound, 1, 0).astype(jnp.int32)
    return count


def doc_array(bounds, first, shape, dim):
    positions = first + lax.broadcasted_iota(jnp.int32, shape, dim)
    count = jnp.zeros(shape, jnp.int32)
    for bound in bounds:
        count = count + jnp.where(positions >= bound, 1, 0)
    return count


def alive_and_trailing(bounds, first, rows, columns):
    docs = doc_array(bounds, first, (rows, columns), 0)
    before = jnp.where(first > 0, doc_scalar(bounds, first - 1), -1)
    last = doc_scalar(bounds, first + rows - 1)
    living = jnp.where(docs == before, 1.0, 0.0).astype(F32)
    trailing = jnp.where(docs == last, 1.0, 0.0).astype(F32)
    return living, trailing


def running_sum(gates):
    rows = gates.shape[0]
    lower = lax.broadcasted_iota(jnp.int32, (rows, rows), 0) >= lax.broadcasted_iota(
        jnp.int32, (rows, rows), 1
    )
    return dot(jnp.where(lower, 1.0, 0.0).astype(BF16), gates, NN)


def states_kernel(n, peers, lens, q, k, v, gates, cot, weight, *outs):
    grad_o, fwd_o, bwd_o, decay_o = outs[:4]
    tokens = q.shape[0]
    if len(outs) > 4:
        cot_own, cot_send = outs[4:]
        dp = lax.axis_index("dp")
        columns = cot.shape[1] // (n * peers)

        @pl.when(pl.program_id(0) == 0)
        def _():
            for c in range(n):
                to = slice(c * columns, (c + 1) * columns)
                for s in range(peers):
                    start = (c * peers + lax.rem(dp + s, peers)) * columns
                    part = cot[:, pl.ds(pl.multiple_of(start, columns), columns)]
                    if s == 0:
                        cot_own[:, to] = part
                    else:
                        cot_send[s - 1, :, to] = part.astype(F32)

    bounds = bounds_of(lens)
    first = lax.axis_index("ctx") * tokens
    grad = dot(cot[...], weight[...], NT)
    grad_o[...] = grad
    cumulative = running_sum(gates[...])
    end = cumulative[tokens - 1 :, :]
    living, trailing = alive_and_trailing(bounds, first, tokens, KEY)
    tail = k[...].astype(F32) * jnp.exp(end - cumulative) * trailing
    alive = q[...].astype(F32) * SCALE * jnp.exp(cumulative) * living
    fwd_o[...] = product(whole(v[...]), split(tail), TN)
    bwd_o[...] = product(split(grad), split(alive), TN)
    decay_o[...] = (jnp.exp(end) * living[tokens - 1 :, :])[None]


def main_kernel(
    n, peers, pieces, norm,
    lens, q, k, v, gates, grad, fwd, bwd, decay, cot_own, cot_send,
    q_o, k_o, v_o, out,
    f_send, b_send, f_recv, b_recv, cum_s, attn_l, dq_l, dk_l, dv_l, fwd_c, bwd_c,
    cot_in, attn, attn_in, part, ring_in,
    chain_sems, cot_sems, attn_send, attn_recv, ring_send, ring_recv,
):
    me, dp, mp = lax.axis_index("ctx"), lax.axis_index("dp"), lax.axis_index("mp")
    tokens = q.shape[0]
    heads = decay.shape[0]
    blocks = tokens // SPAN
    cores = lax.axis_size("mp")
    right, left = lax.rem(me + 1, n), lax.rem(me + n - 1, n)
    others = [lax.rem(dp + s, peers) for s in range(1, peers)]
    mates = [lax.rem(mp + s, cores) for s in range(1, cores)]

    barrier = pltpu.get_barrier_semaphore()
    for other in others:
        pl.semaphore_signal(barrier, inc=1, device_id={"dp": other}, device_id_type=MESH)
    for near in (left, right):
        pl.semaphore_signal(barrier, inc=1, device_id={"ctx": near}, device_id_type=MESH)
    for mate in mates:
        pl.semaphore_signal(barrier, inc=1, device_id={"mp": mate}, device_id_type=MESH)
    pl.semaphore_wait(barrier, len(others) + 2 + len(mates))

    share = tokens // cores

    def remote(src, dst, send_sem, recv_sem, to):
        return pltpu.make_async_remote_copy(
            src_ref=src, dst_ref=dst, send_sem=send_sem, recv_sem=recv_sem,
            device_id=to, device_id_type=MESH,
        )

    def cot_copy(p):
        rows = pl.ds(pl.multiple_of(mp * share, share), share)
        return remote(
            cot_send.at[p, rows], cot_in.at[p, rows], cot_sems.at[0, p, 0], cot_sems.at[1, p, 0],
            {"dp": others[p]},
        )

    def mate_copy(p, m):
        rows = pl.ds(pl.multiple_of(mp * share, share), share)
        return remote(
            cot_in.at[p, rows], cot_in.at[p, rows], cot_sems.at[0, p, m + 1],
            cot_sems.at[1, p, m + 1], {"mp": mates[m]},
        )

    for p in range(peers - 1):
        cot_copy(p).start()

    rows_each = fwd.shape[0] // pieces
    per_head = pieces // heads
    has_left, has_right = me > 0, me < n - 1

    def chain_copy(c, send, recv, base, to):
        at = pl.ds(pl.multiple_of(c * rows_each, rows_each), rows_each)
        return remote(
            send.at[at], recv.at[at], chain_sems.at[base, c], chain_sems.at[base + 1, c], {"ctx": to}
        )

    def chain_piece(c, own, send, recv, base, has_source, has_target, to):
        at = pl.ds(pl.multiple_of(c * rows_each, rows_each), rows_each)

        @pl.when(has_source)
        def _():
            chain_copy(c, send, recv, base, to).wait_recv()

        @pl.when(jnp.logical_not(has_source))
        def _():
            recv[at, :] = jnp.zeros((rows_each, KEY), F32)

        @pl.when(has_target)
        def _():
            send[at, :] = decay[c // per_head] * recv[at, :] + own[at, :]
            chain_copy(c, send, recv, base, to).start()

    def slot(s, carry):
        up = s - SKEW * me
        down = s - SKEW * (n - 1 - me)

        @pl.when((up >= 0) & (up < pieces))
        def _():
            chain_piece(up, fwd, f_send, f_recv, 0, has_left, has_right, right)

        @pl.when((down >= 0) & (down < pieces))
        def _():
            chain_piece(down, bwd, b_send, b_recv, 2, has_right, has_left, left)

        return carry

    bounds = bounds_of(lens)
    device_first = me * tokens

    def of_head(h, n_block):
        at = slice(n_block * SPAN, (n_block + 1) * SPAN)
        return at, slice(h * KEY, (h + 1) * KEY), slice(h * VAL, (h + 1) * VAL)

    def inner(h, n_block):
        at, hk, hv = of_head(h, n_block)
        first = device_first + n_block * SPAN
        cumulative = running_sum(gates[at, hk])
        cum_s[at, hk] = cumulative
        growth = jnp.exp(cumulative)
        shrink = jnp.exp(-cumulative)
        end = cumulative[SPAN - 1 :, :]
        living, trailing = alive_and_trailing(bounds, first, SPAN, KEY)
        rows = lax.broadcasted_iota(jnp.int32, (SPAN, SPAN), 0)
        columns = lax.broadcasted_iota(jnp.int32, (SPAN, SPAN), 1)
        same = doc_array(bounds, first, (SPAN, SPAN), 0) == doc_array(bounds, first, (SPAN, SPAN), 1)
        mask = jnp.where((rows >= columns) & same, 1.0, 0.0).astype(F32)
        value = whole(v[at, hv])
        key = k[at, hk].astype(F32)
        grown = q[at, hk].astype(F32) * SCALE * growth
        grown_p, shrunk_p, grad_p = split(grown), split(key * shrink), split(grad[at, hv])
        scores = split(product(grown_p, shrunk_p, NT) * mask)
        mixing = split(product(grad_p, value, NT) * mask)
        attn_l[at, hv] = product(scores, value, NN)
        dq_l[at, hk] = product(mixing, shrunk_p, NN)
        dk_l[at, hk] = shrink * product(mixing, grown_p, TN)
        dv_l[at, hv] = product(scores, grad_p, TN)
        if n_block < blocks - 1:
            tail = split(key * jnp.exp(end - cumulative) * trailing)
            fwd_c[h, n_block] = product(value, tail, TN)
        if n_block > 0:
            bwd_c[h, n_block - 1] = product(grad_p, split(grown * living), TN)

    units = [(h, b) for h in range(heads) for b in range(blocks)]
    slots = pieces + SKEW * (n - 1)
    done = 0
    for u, (h, b) in enumerate(units):
        until = (u + 1) * slots // len(units)
        lax.fori_loop(done, until, slot, 0)
        done = until
        inner(h, b)

    for p in range(peers - 1):
        cot_copy(p).wait_recv()
        for m in range(cores - 1):
            mate_copy(p, m).start()

    def attn_copy(p, j):
        return remote(
            attn.at[j], attn_in.at[p, j], attn_send.at[p, j], attn_recv.at[p, j], {"dp": others[p]}
        )

    parts_of_head = VAL // PIECE

    def forward(h):
        state = f_recv[h * VAL : (h + 1) * VAL, :]
        for b in range(blocks):
            at, hk, hv = of_head(h, b)
            cumulative = cum_s[at, hk]
            growth = jnp.exp(cumulative)
            living, _ = alive_and_trailing(bounds, device_first + b * SPAN, SPAN, KEY)
            alive = split(q[at, hk].astype(F32) * SCALE * growth * living)
            state_p = split(state)
            total = attn_l[at, hv] + product(alive, state_p, NT)
            total = total.astype(BF16).astype(F32)
            for p in range(parts_of_head):
                attn[h * parts_of_head + p, at, :] = total[:, p * PIECE : (p + 1) * PIECE]
            dq = dq_l[at, hk] + living * product(split(grad[at, hv]), state_p, NN)
            q_o[at, hk] = (growth * dq * SCALE).astype(BF16)
            if b < blocks - 1:
                keep = growth[SPAN - 1 :, :] * living[SPAN - 1 :, :]
                state = keep * state + fwd_c[h, b]

    def backward(h):
        state = b_recv[h * VAL : (h + 1) * VAL, :]
        for b in reversed(range(blocks)):
            at, hk, hv = of_head(h, b)
            cumulative = cum_s[at, hk]
            end = cumulative[SPAN - 1 :, :]
            living, trailing = alive_and_trailing(bounds, device_first + b * SPAN, SPAN, KEY)
            from_end = jnp.exp(end - cumulative) * trailing
            tail = split(k[at, hk].astype(F32) * from_end)
            state_p = split(state)
            dk = dk_l[at, hk] + from_end * product(whole(v[at, hv]), state_p, NN)
            k_o[at, hk] = dk.astype(BF16)
            v_o[at, hv] = (dv_l[at, hv] + product(tail, state_p, NT)).astype(BF16)
            if b > 0:
                keep = jnp.exp(end) * living[SPAN - 1 :, :]
                state = keep * state + bwd_c[h, b - 1]

    for h in range(heads):
        forward(h)
        for j in range(h * parts_of_head, (h + 1) * parts_of_head):
            for p in range(peers - 1):
                attn_copy(p, j).start()
    for h in range(heads):
        backward(h)

    half = PIECE // 2
    columns = out.shape[1]
    parts = attn.shape[0]

    def chunk_at(way, step):
        if way == 0:
            return lax.rem(me - 1 - step + 2 * n, n)
        return lax.rem(me + 1 + step, n)

    def ring_copy(j, way, step):
        return remote(
            part.at[j, chunk_at(way, step), pl.ds(way * half, half)],
            ring_in.at[j, way, step],
            ring_send.at[j, way, step],
            ring_recv.at[j, way, step],
            {"ctx": right if way == 0 else left},
        )

    for p in range(peers - 1):
        for m in range(cores - 1):
            mate_copy(p, m).wait_recv()

    def multiply(j):
        total = dot(attn[j].astype(BF16), cot_own[...], TN)
        for p in range(peers - 1):
            attn_copy(p, j).wait_recv()
            total = total + dot(attn_in[p, j].astype(BF16), cot_in[p].astype(BF16), TN)
        for c in range(n):
            part[j, c] = total[:, c * columns : (c + 1) * columns]
        for way in range(2):
            ring_copy(j, way, 0).start()

    def pass_on(j, step):
        for way in range(2):
            ring_copy(j, way, step - 1).wait_recv()
            c = chunk_at(way, step)
            rows = pl.ds(way * half, half)
            total = part[j, c, rows, :] + ring_in[j, way, step - 1]
            if step < n - 1:
                part[j, c, rows, :] = total
                ring_copy(j, way, step).start()
            else:
                out[pl.ds(j * PIECE + way * half, half), :] = total * norm

    for t in range(parts + n - 1):
        if t < parts:
            multiply(t)
        for j in range(parts):
            if 1 <= t - j <= n - 1:
                pass_on(j, t - j)

    def finish(c, carry):
        @pl.when(has_right)
        def _():
            chain_copy(c, f_send, f_recv, 0, right).wait_send()

        @pl.when(has_left)
        def _():
            chain_copy(c, b_send, b_recv, 2, left).wait_send()

        return carry

    lax.fori_loop(0, pieces, finish, 0)
    for p in range(peers - 1):
        cot_copy(p).wait_send()
        for m in range(cores - 1):
            mate_copy(p, m).wait_send()
    for j in range(parts):
        for p in range(peers - 1):
            attn_copy(p, j).wait_send()
        for way in range(2):
            for step in range(n - 1):
                ring_copy(j, way, step).wait_send()


def params(**more):
    return pltpu.CompilerParams(vmem_limit_bytes=VMEM_BYTES, **more)


def per_device(queries, key_vectors, value_vectors, log_gates, doc_lengths, cotangent, out_weight):
    q, k, v, gates, cot = (x[0] for x in (queries, key_vectors, value_vectors, log_gates, cotangent))
    tokens, width = cot.shape
    heads = out_weight.shape[0] // VAL
    n, peers = lax.axis_size("ctx"), lax.axis_size("dp")
    dp = lax.axis_index("dp")
    columns = width // (n * peers)
    smem = pl.BlockSpec(memory_space=pltpu.SMEM)

    in_kernel = columns % 128 == 0
    spread = n * columns

    def head_block(rows, cols):
        return pl.BlockSpec((rows, cols), lambda h: (0, h))

    def head_rows(rows, cols):
        return pl.BlockSpec((rows, cols), lambda h: (h, 0))

    grad, fwd, bwd, decay, *cots = pl.pallas_call(
        functools.partial(states_kernel, n, peers),
        grid=(heads,),
        in_specs=[
            smem,
            head_block(tokens, KEY),
            head_block(tokens, KEY),
            head_block(tokens, VAL),
            head_block(tokens, KEY),
            pl.BlockSpec((tokens, width), lambda h: (0, 0)),
            head_rows(VAL, width),
        ],
        out_specs=[
            head_block(tokens, VAL),
            head_rows(VAL, KEY),
            head_rows(VAL, KEY),
            pl.BlockSpec((1, 1, KEY), lambda h: (h, 0, 0)),
        ]
        + [
            pl.BlockSpec((tokens, spread), lambda h: (0, 0)),
            pl.BlockSpec((peers - 1, tokens, spread), lambda h: (0, 0, 0)),
        ]
        * in_kernel,
        out_shape=[
            jax.ShapeDtypeStruct((tokens, heads * VAL), F32),
            jax.ShapeDtypeStruct((heads * VAL, KEY), F32),
            jax.ShapeDtypeStruct((heads * VAL, KEY), F32),
            jax.ShapeDtypeStruct((heads, 1, KEY), F32),
        ]
        + [
            jax.ShapeDtypeStruct((tokens, spread), BF16),
            jax.ShapeDtypeStruct((peers - 1, tokens, spread), F32),
        ]
        * in_kernel,
        compiler_params=params(),
        cost_estimate=pl.CostEstimate(flops=6 * 10**9, bytes_accessed=14 << 20, transcendentals=0),
        name="states",
    )(doc_lengths, q, k, v, gates, cot, out_weight)

    if in_kernel:
        cot_own, cot_send = cots
    else:
        parted = cot.reshape(tokens, n, peers, columns)
        shares = [
            lax.dynamic_index_in_dim(parted, lax.rem(dp + s, peers), axis=2, keepdims=False).reshape(
                tokens, spread
            )
            for s in range(peers)
        ]
        cot_own, cot_send = shares[0], jnp.stack(shares[1:]).astype(F32)

    pieces = 8 * heads
    vmem = pl.BlockSpec(memory_space=pltpu.VMEM)
    states = (heads * VAL, KEY)
    keys, values = (tokens, heads * KEY), (tokens, heads * VAL)
    parts = heads * VAL // PIECE
    blocks = tokens // SPAN
    cores = lax.axis_size("mp")
    dma = pltpu.SemaphoreType.DMA
    norm = 1.0 / math.sqrt(peers * n * tokens)
    scratch = (
        [states] * 4
        + [keys, values, keys, keys, values]
        + [(heads, blocks - 1, VAL, KEY)] * 2
        + [
            (peers - 1, tokens, spread),
            (parts, tokens, PIECE),
            (peers - 1, parts, tokens, PIECE),
            (parts, n, PIECE, columns),
            (parts, 2, n - 1, PIECE // 2, columns),
        ]
    )
    query_grad, key_grad, value_grad, weight_grad = pl.pallas_call(
        functools.partial(main_kernel, n, peers, pieces, norm),
        in_specs=[smem] + [vmem] * 10,
        out_specs=[vmem] * 4,
        out_shape=[
            jax.ShapeDtypeStruct(keys, BF16),
            jax.ShapeDtypeStruct(keys, BF16),
            jax.ShapeDtypeStruct(values, BF16),
            jax.ShapeDtypeStruct((heads * VAL, columns), F32),
        ],
        scratch_shapes=[pltpu.VMEM(shape, F32) for shape in scratch]
        + [
            dma((4, pieces)),
            dma((2, peers - 1, cores)),
            dma((peers - 1, parts)),
            dma((peers - 1, parts)),
            dma((parts, 2, n - 1)),
            dma((parts, 2, n - 1)),
        ],
        compiler_params=params(collective_id=0, has_side_effects=True),
        cost_estimate=pl.CostEstimate(flops=10**10, bytes_accessed=64 << 20, transcendentals=0),
        name="main",
    )(doc_lengths, q, k, v, gates, grad, fwd, bwd, decay, cot_own, cot_send)
    return (query_grad[None], key_grad[None], value_grad[None], weight_grad)


def solution(mesh):
    batch = ("groups", "dp")
    return jax.shard_map(
        per_device,
        mesh=mesh,
        in_specs=(
            P(batch, "ctx", "mp"),
            P(batch, "ctx", "mp"),
            P(batch, "ctx", "mp"),
            P(batch, "ctx", "mp"),
            P(batch, None),
            P(batch, "ctx", None),
            P("mp", None),
        ),
        out_specs=(
            P(batch, "ctx", "mp"),
            P(batch, "ctx", "mp"),
            P(batch, "ctx", "mp"),
            P(("groups", "mp"), ("ctx", "dp")),
        ),
        check_vma=False,
    )
```

```python
import functools
import math

import jax
import jax.numpy as jnp
from jax import lax
from jax.experimental import pallas as pl
from jax.experimental.pallas import tpu as pltpu
from jax.sharding import PartitionSpec as P

KEY = 256
VAL = 512
SPAN = 128
SKEW = 3
PIECE = 256
SCALE = KEY ** (-0.5)
VMEM_BYTES = 60 * 1024 * 1024
MESH = pl.DeviceIdType.MESH
F32 = jnp.float32
BF16 = jnp.bfloat16

NN = (((1,), (0,)), ((), ()))
NT = (((1,), (1,)), ((), ()))
TN = (((0,), (0,)), ((), ()))


def dot(a, b, dims):
    return lax.dot_general(a, b, dims, preferred_element_type=F32)


def split(x):
    high = x.astype(BF16)
    return high, (x - high.astype(F32)).astype(BF16)


def whole(x):
    return x, None


def product(a, b, dims):
    out = dot(a[0], b[0], dims)
    if a[1] is not None:
        out = out + dot(a[1], b[0], dims)
    if b[1] is not None:
        out = out + dot(a[0], b[1], dims)
    return out


def bounds_of(lens_ref):
    bounds, total = [], 0
    for d in range(lens_ref.shape[1]):
        total = total + lens_ref[0, d]
        bounds.append(total)
    return bounds


def doc_scalar(bounds, position):
    count = jnp.int32(0)
    for bound in bounds:
        count = count + jnp.where(position >= bound, 1, 0).astype(jnp.int32)
    return count


def doc_array(bounds, first, shape, dim):
    positions = first + lax.broadcasted_iota(jnp.int32, shape, dim)
    count = jnp.zeros(shape, jnp.int32)
    for bound in bounds:
        count = count + jnp.where(positions >= bound, 1, 0)
    return count


def alive_and_trailing(bounds, first, rows, columns):
    docs = doc_array(bounds, first, (rows, columns), 0)
    before = jnp.where(first > 0, doc_scalar(bounds, first - 1), -1)
    last = doc_scalar(bounds, first + rows - 1)
    living = jnp.where(docs == before, 1.0, 0.0).astype(F32)
    trailing = jnp.where(docs == last, 1.0, 0.0).astype(F32)
    return living, trailing


def running_sum(gates):
    rows = gates.shape[0]
    lower = lax.broadcasted_iota(jnp.int32, (rows, rows), 0) >= lax.broadcasted_iota(
        jnp.int32, (rows, rows), 1
    )
    return dot(jnp.where(lower, 1.0, 0.0).astype(BF16), gates, NN)


def states_kernel(n, peers, lens, q, k, v, gates, cot, weight, *outs):
    grad_o, fwd_o, bwd_o, decay_o = outs[:4]
    tokens = q.shape[0]
    if len(outs) > 4:
        cot_own, cot_send = outs[4:]
        dp = lax.axis_index("dp")
        columns = cot.shape[1] // (n * peers)

        @pl.when(pl.program_id(0) == 0)
        def _():
            for c in range(n):
                to = slice(c * columns, (c + 1) * columns)
                for s in range(peers):
                    start = (c * peers + lax.rem(dp + s, peers)) * columns
                    part = cot[:, pl.ds(pl.multiple_of(start, columns), columns)]
                    if s == 0:
                        cot_own[:, to] = part
                    else:
                        cot_send[s - 1, :, to] = part.astype(F32)

    bounds = bounds_of(lens)
    first = lax.axis_index("ctx") * tokens
    grad = dot(cot[...], weight[...], NT)
    grad_o[...] = grad
    cumulative = running_sum(gates[...])
    end = cumulative[tokens - 1 :, :]
    living, trailing = alive_and_trailing(bounds, first, tokens, KEY)
    tail = k[...].astype(F32) * jnp.exp(end - cumulative) * trailing
    alive = q[...].astype(F32) * SCALE * jnp.exp(cumulative) * living
    fwd_o[...] = product(whole(v[...]), split(tail), TN)
    bwd_o[...] = product(split(grad), split(alive), TN)
    decay_o[...] = (jnp.exp(end) * living[tokens - 1 :, :])[None]


def main_kernel(
    n, peers, pieces, norm,
    lens, q, k, v, gates, grad, fwd, bwd, decay, cot_own, cot_send,
    q_o, k_o, v_o, out,
    f_send, b_send, f_recv, b_recv, cum_s, attn_l, dq_l, dk_l, dv_l, fwd_c, bwd_c,
    cot_in, attn, attn_in, part, line_in,
    chain_sems, cot_sems, attn_send, attn_recv, line_send, line_recv,
):
    me, dp, mp = lax.axis_index("ctx"), lax.axis_index("dp"), lax.axis_index("mp")
    tokens = q.shape[0]
    heads = decay.shape[0]
    blocks = tokens // SPAN
    cores = lax.axis_size("mp")
    right, left = lax.rem(me + 1, n), lax.rem(me + n - 1, n)
    others = [lax.rem(dp + s, peers) for s in range(1, peers)]
    mates = [lax.rem(mp + s, cores) for s in range(1, cores)]

    barrier = pltpu.get_barrier_semaphore()
    for other in others:
        pl.semaphore_signal(barrier, inc=1, device_id={"dp": other}, device_id_type=MESH)
    for near in (left, right):
        pl.semaphore_signal(barrier, inc=1, device_id={"ctx": near}, device_id_type=MESH)
    for mate in mates:
        pl.semaphore_signal(barrier, inc=1, device_id={"mp": mate}, device_id_type=MESH)
    pl.semaphore_wait(barrier, len(others) + 2 + len(mates))

    share = tokens // cores

    def remote(src, dst, send_sem, recv_sem, to):
        return pltpu.make_async_remote_copy(
            src_ref=src, dst_ref=dst, send_sem=send_sem, recv_sem=recv_sem,
            device_id=to, device_id_type=MESH,
        )

    def cot_copy(p):
        rows = pl.ds(pl.multiple_of(mp * share, share), share)
        return remote(
            cot_send.at[p, rows], cot_in.at[p, rows], cot_sems.at[0, p, 0], cot_sems.at[1, p, 0],
            {"dp": others[p]},
        )

    def mate_copy(p, m):
        rows = pl.ds(pl.multiple_of(mp * share, share), share)
        return remote(
            cot_in.at[p, rows], cot_in.at[p, rows], cot_sems.at[0, p, m + 1],
            cot_sems.at[1, p, m + 1], {"mp": mates[m]},
        )

    for p in range(peers - 1):
        cot_copy(p).start()

    rows_each = fwd.shape[0] // pieces
    per_head = pieces // heads
    has_left, has_right = me > 0, me < n - 1

    def chain_copy(c, send, recv, base, to):
        at = pl.ds(pl.multiple_of(c * rows_each, rows_each), rows_each)
        return remote(
            send.at[at], recv.at[at], chain_sems.at[base, c], chain_sems.at[base + 1, c], {"ctx": to}
        )

    def chain_piece(c, own, send, recv, base, has_source, has_target, to):
        at = pl.ds(pl.multiple_of(c * rows_each, rows_each), rows_each)

        @pl.when(has_source)
        def _():
            chain_copy(c, send, recv, base, to).wait_recv()

        @pl.when(jnp.logical_not(has_source))
        def _():
            recv[at, :] = jnp.zeros((rows_each, KEY), F32)

        @pl.when(has_target)
        def _():
            send[at, :] = decay[c // per_head] * recv[at, :] + own[at, :]
            chain_copy(c, send, recv, base, to).start()

    def slot(s, carry):
        up = s - SKEW * me
        down = s - SKEW * (n - 1 - me)

        @pl.when((up >= 0) & (up < pieces))
        def _():
            chain_piece(up, fwd, f_send, f_recv, 0, has_left, has_right, right)

        @pl.when((down >= 0) & (down < pieces))
        def _():
            chain_piece(down, bwd, b_send, b_recv, 2, has_right, has_left, left)

        return carry

    bounds = bounds_of(lens)
    device_first = me * tokens

    def of_head(h, n_block):
        at = slice(n_block * SPAN, (n_block + 1) * SPAN)
        return at, slice(h * KEY, (h + 1) * KEY), slice(h * VAL, (h + 1) * VAL)

    def inner(h, n_block):
        at, hk, hv = of_head(h, n_block)
        first = device_first + n_block * SPAN
        cumulative = running_sum(gates[at, hk])
        cum_s[at, hk] = cumulative
        growth = jnp.exp(cumulative)
        shrink = jnp.exp(-cumulative)
        end = cumulative[SPAN - 1 :, :]
        living, trailing = alive_and_trailing(bounds, first, SPAN, KEY)
        rows = lax.broadcasted_iota(jnp.int32, (SPAN, SPAN), 0)
        columns = lax.broadcasted_iota(jnp.int32, (SPAN, SPAN), 1)
        same = doc_array(bounds, first, (SPAN, SPAN), 0) == doc_array(bounds, first, (SPAN, SPAN), 1)
        mask = jnp.where((rows >= columns) & same, 1.0, 0.0).astype(F32)
        value = whole(v[at, hv])
        key = k[at, hk].astype(F32)
        grown = q[at, hk].astype(F32) * SCALE * growth
        grown_p, shrunk_p, grad_p = split(grown), split(key * shrink), split(grad[at, hv])
        scores = split(product(grown_p, shrunk_p, NT) * mask)
        mixing = split(product(grad_p, value, NT) * mask)
        attn_l[at, hv] = product(scores, value, NN)
        dq_l[at, hk] = product(mixing, shrunk_p, NN)
        dk_l[at, hk] = shrink * product(mixing, grown_p, TN)
        dv_l[at, hv] = product(scores, grad_p, TN)
        if n_block < blocks - 1:
            tail = split(key * jnp.exp(end - cumulative) * trailing)
            fwd_c[h, n_block] = product(value, tail, TN)
        if n_block > 0:
            bwd_c[h, n_block - 1] = product(grad_p, split(grown * living), TN)

    def attn_copy(p, j):
        return remote(
            attn.at[j], attn_in.at[p, j], attn_send.at[p, j], attn_recv.at[p, j], {"dp": others[p]}
        )

    parts_of_head = VAL // PIECE

    def forward(h):
        state = f_recv[h * VAL : (h + 1) * VAL, :]
        for b in range(blocks):
            at, hk, hv = of_head(h, b)
            cumulative = cum_s[at, hk]
            growth = jnp.exp(cumulative)
            living, _ = alive_and_trailing(bounds, device_first + b * SPAN, SPAN, KEY)
            alive = split(q[at, hk].astype(F32) * SCALE * growth * living)
            state_p = split(state)
            total = attn_l[at, hv] + product(alive, state_p, NT)
            total = total.astype(BF16).astype(F32)
            for p in range(parts_of_head):
                attn[h * parts_of_head + p, at, :] = total[:, p * PIECE : (p + 1) * PIECE]
            dq = dq_l[at, hk] + living * product(split(grad[at, hv]), state_p, NN)
            q_o[at, hk] = (growth * dq * SCALE).astype(BF16)
            if b < blocks - 1:
                keep = growth[SPAN - 1 :, :] * living[SPAN - 1 :, :]
                state = keep * state + fwd_c[h, b]

    def backward(h):
        state = b_recv[h * VAL : (h + 1) * VAL, :]
        for b in reversed(range(blocks)):
            at, hk, hv = of_head(h, b)
            cumulative = cum_s[at, hk]
            end = cumulative[SPAN - 1 :, :]
            living, trailing = alive_and_trailing(bounds, device_first + b * SPAN, SPAN, KEY)
            from_end = jnp.exp(end - cumulative) * trailing
            tail = split(k[at, hk].astype(F32) * from_end)
            state_p = split(state)
            dk = dk_l[at, hk] + from_end * product(whole(v[at, hv]), state_p, NN)
            k_o[at, hk] = dk.astype(BF16)
            v_o[at, hv] = (dv_l[at, hv] + product(tail, state_p, NT)).astype(BF16)
            if b > 0:
                keep = jnp.exp(end) * living[SPAN - 1 :, :]
                state = keep * state + bwd_c[h, b - 1]

    done, waiting = 0, [(h, b) for h in range(heads) for b in range(blocks)]
    for h in range(heads):
        target = (h + 1) * per_head + SKEW * (n - 1)
        own = [u for u in waiting if u[0] <= h]
        more = [u for u in waiting if u[0] > h][: blocks // 2]
        waiting = [u for u in waiting if u not in own and u not in more]
        start = done
        for i, unit in enumerate(own + more):
            until = start + (i + 1) * (target - start) // len(own + more)
            lax.fori_loop(done, until, slot, 0)
            done = until
            inner(*unit)
        lax.fori_loop(done, target, slot, 0)
        done = target
        forward(h)
        for j in range(h * parts_of_head, (h + 1) * parts_of_head):
            for p in range(peers - 1):
                attn_copy(p, j).start()

    for p in range(peers - 1):
        cot_copy(p).wait_recv()
        for m in range(cores - 1):
            mate_copy(p, m).start()

    columns = out.shape[1]
    parts = attn.shape[0]

    def line_copy(j, c, up):
        place = c if up else jnp.where(me - 1 == c, n, c)
        return remote(
            part.at[j, c], line_in.at[j, place], line_send.at[j, c], line_recv.at[j, place],
            {"ctx": right if up else left},
        )

    def arrival(j, place, up):
        return remote(
            part.at[j, 0], line_in.at[j, place], line_send.at[j, 0], line_recv.at[j, place],
            {"ctx": right if up else left},
        )

    for p in range(peers - 1):
        for m in range(cores - 1):
            mate_copy(p, m).wait_recv()

    def multiply(j):
        total = dot(attn[j].astype(BF16), cot_own[...], TN)
        for p in range(peers - 1):
            attn_copy(p, j).wait_recv()
            total = total + dot(attn_in[p, j].astype(BF16), cot_in[p].astype(BF16), TN)
        for c in range(n):
            part[j, c] = total[:, c * columns : (c + 1) * columns]

    def sent(j, c):
        return remote(
            part.at[j, c], line_in.at[j, c], line_send.at[j, c], line_recv.at[j, c], {"ctx": right}
        )

    def add_and_send(j, c, up, has_source):
        @pl.when(has_source)
        def _():
            arrival(j, c, up).wait_recv()
            part[j, c] = part[j, c] + line_in[j, c]

        line_copy(j, c, up).start()

    def pass_on(j):
        for c in reversed(range(1, n)):

            @pl.when(me < c)
            def _():
                add_and_send(j, c, True, has_left)

        for c in range(n - 1):

            @pl.when(me > c)
            def _():
                add_and_send(j, c, False, has_right)

    def settle(j):
        at = pl.ds(j * PIECE, PIECE)
        out[at, :] = part[j, me] * norm

        @pl.when(has_left)
        def _():
            arrival(j, me, True).wait_recv()
            out[at, :] = out[at, :] + line_in[j, me] * norm

        @pl.when(has_right)
        def _():
            arrival(j, n, False).wait_recv()
            out[at, :] = out[at, :] + line_in[j, n] * norm

    for j in range(parts):
        multiply(j)
        pass_on(j)
        if j < heads:
            backward(j)
    for j in range(parts):
        settle(j)

    def finish(c, carry):
        @pl.when(has_right)
        def _():
            chain_copy(c, f_send, f_recv, 0, right).wait_send()

        @pl.when(has_left)
        def _():
            chain_copy(c, b_send, b_recv, 2, left).wait_send()

        return carry

    lax.fori_loop(0, pieces, finish, 0)
    for p in range(peers - 1):
        cot_copy(p).wait_send()
        for m in range(cores - 1):
            mate_copy(p, m).wait_send()
    for j in range(parts):
        for p in range(peers - 1):
            attn_copy(p, j).wait_send()
        for c in range(n):

            @pl.when(me != c)
            def _():
                sent(j, c).wait_send()


def params(**more):
    return pltpu.CompilerParams(vmem_limit_bytes=VMEM_BYTES, **more)


def per_device(queries, key_vectors, value_vectors, log_gates, doc_lengths, cotangent, out_weight):
    q, k, v, gates, cot = (x[0] for x in (queries, key_vectors, value_vectors, log_gates, cotangent))
    tokens, width = cot.shape
    heads = out_weight.shape[0] // VAL
    n, peers = lax.axis_size("ctx"), lax.axis_size("dp")
    dp = lax.axis_index("dp")
    columns = width // (n * peers)
    smem = pl.BlockSpec(memory_space=pltpu.SMEM)

    in_kernel = columns % 128 == 0
    spread = n * columns

    def head_block(rows, cols):
        return pl.BlockSpec((rows, cols), lambda h: (0, h))

    def head_rows(rows, cols):
        return pl.BlockSpec((rows, cols), lambda h: (h, 0))

    grad, fwd, bwd, decay, *cots = pl.pallas_call(
        functools.partial(states_kernel, n, peers),
        grid=(heads,),
        in_specs=[
            smem,
            head_block(tokens, KEY),
            head_block(tokens, KEY),
            head_block(tokens, VAL),
            head_block(tokens, KEY),
            pl.BlockSpec((tokens, width), lambda h: (0, 0)),
            head_rows(VAL, width),
        ],
        out_specs=[
            head_block(tokens, VAL),
            head_rows(VAL, KEY),
            head_rows(VAL, KEY),
            pl.BlockSpec((1, 1, KEY), lambda h: (h, 0, 0)),
        ]
        + [
            pl.BlockSpec((tokens, spread), lambda h: (0, 0)),
            pl.BlockSpec((peers - 1, tokens, spread), lambda h: (0, 0, 0)),
        ]
        * in_kernel,
        out_shape=[
            jax.ShapeDtypeStruct((tokens, heads * VAL), F32),
            jax.ShapeDtypeStruct((heads * VAL, KEY), F32),
            jax.ShapeDtypeStruct((heads * VAL, KEY), F32),
            jax.ShapeDtypeStruct((heads, 1, KEY), F32),
        ]
        + [
            jax.ShapeDtypeStruct((tokens, spread), BF16),
            jax.ShapeDtypeStruct((peers - 1, tokens, spread), F32),
        ]
        * in_kernel,
        compiler_params=params(),
        cost_estimate=pl.CostEstimate(flops=6 * 10**9, bytes_accessed=14 << 20, transcendentals=0),
        name="states",
    )(doc_lengths, q, k, v, gates, cot, out_weight)

    if in_kernel:
        cot_own, cot_send = cots
    else:
        parted = cot.reshape(tokens, n, peers, columns)
        shares = [
            lax.dynamic_index_in_dim(parted, lax.rem(dp + s, peers), axis=2, keepdims=False).reshape(
                tokens, spread
            )
            for s in range(peers)
        ]
        cot_own, cot_send = shares[0], jnp.stack(shares[1:]).astype(F32)

    pieces = 8 * heads
    vmem = pl.BlockSpec(memory_space=pltpu.VMEM)
    states = (heads * VAL, KEY)
    keys, values = (tokens, heads * KEY), (tokens, heads * VAL)
    parts = heads * VAL // PIECE
    blocks = tokens // SPAN
    cores = lax.axis_size("mp")
    dma = pltpu.SemaphoreType.DMA
    norm = 1.0 / math.sqrt(peers * n * tokens)
    scratch = (
        [states] * 4
        + [keys, values, keys, keys, values]
        + [(heads, blocks - 1, VAL, KEY)] * 2
        + [
            (peers - 1, tokens, spread),
            (parts, tokens, PIECE),
            (peers - 1, parts, tokens, PIECE),
            (parts, n, PIECE, columns),
            (parts, n + 1, PIECE, columns),
        ]
    )
    query_grad, key_grad, value_grad, weight_grad = pl.pallas_call(
        functools.partial(main_kernel, n, peers, pieces, norm),
        in_specs=[smem] + [vmem] * 10,
        out_specs=[vmem] * 4,
        out_shape=[
            jax.ShapeDtypeStruct(keys, BF16),
            jax.ShapeDtypeStruct(keys, BF16),
            jax.ShapeDtypeStruct(values, BF16),
            jax.ShapeDtypeStruct((heads * VAL, columns), F32),
        ],
        scratch_shapes=[pltpu.VMEM(shape, F32) for shape in scratch]
        + [
            dma((4, pieces)),
            dma((2, peers - 1, cores)),
            dma((peers - 1, parts)),
            dma((peers - 1, parts)),
            dma((parts, n)),
            dma((parts, n + 1)),
        ],
        compiler_params=params(collective_id=0, has_side_effects=True),
        cost_estimate=pl.CostEstimate(flops=10**10, bytes_accessed=64 << 20, transcendentals=0),
        name="main",
    )(doc_lengths, q, k, v, gates, grad, fwd, bwd, decay, cot_own, cot_send)
    return (query_grad[None], key_grad[None], value_grad[None], weight_grad)


def solution(mesh):
    batch = ("groups", "dp")
    return jax.shard_map(
        per_device,
        mesh=mesh,
        in_specs=(
            P(batch, "ctx", "mp"),
            P(batch, "ctx", "mp"),
            P(batch, "ctx", "mp"),
            P(batch, "ctx", "mp"),
            P(batch, None),
            P(batch, "ctx", None),
            P("mp", None),
        ),
        out_specs=(
            P(batch, "ctx", "mp"),
            P(batch, "ctx", "mp"),
            P(batch, "ctx", "mp"),
            P(("groups", "mp"), ("ctx", "dp")),
        ),
        check_vma=False,
    )
```

```python
import functools
import math

import jax
import jax.numpy as jnp
from jax import lax
from jax.experimental import pallas as pl
from jax.experimental.pallas import tpu as pltpu
from jax.sharding import PartitionSpec as P

KEY = 256
VAL = 512
SPAN = 128
SKEW = 3
PIECE = 256
SCALE = KEY ** (-0.5)
VMEM_BYTES = 60 * 1024 * 1024
MESH = pl.DeviceIdType.MESH
F32 = jnp.float32
BF16 = jnp.bfloat16

NN = (((1,), (0,)), ((), ()))
NT = (((1,), (1,)), ((), ()))
TN = (((0,), (0,)), ((), ()))


def dot(a, b, dims):
    return lax.dot_general(a, b, dims, preferred_element_type=F32)


def split(x):
    high = x.astype(BF16)
    return high, (x - high.astype(F32)).astype(BF16)


def whole(x):
    return x, None


def product(a, b, dims):
    out = dot(a[0], b[0], dims)
    if a[1] is not None:
        out = out + dot(a[1], b[0], dims)
    if b[1] is not None:
        out = out + dot(a[0], b[1], dims)
    return out


def bounds_of(lens_ref):
    bounds, total = [], 0
    for d in range(lens_ref.shape[1]):
        total = total + lens_ref[0, d]
        bounds.append(total)
    return bounds


def doc_scalar(bounds, position):
    count = jnp.int32(0)
    for bound in bounds:
        count = count + jnp.where(position >= bound, 1, 0).astype(jnp.int32)
    return count


def doc_array(bounds, first, shape, dim):
    positions = first + lax.broadcasted_iota(jnp.int32, shape, dim)
    count = jnp.zeros(shape, jnp.int32)
    for bound in bounds:
        count = count + jnp.where(positions >= bound, 1, 0)
    return count


def alive_and_trailing(bounds, first, rows, columns):
    docs = doc_array(bounds, first, (rows, columns), 0)
    before = jnp.where(first > 0, doc_scalar(bounds, first - 1), -1)
    last = doc_scalar(bounds, first + rows - 1)
    living = jnp.where(docs == before, 1.0, 0.0).astype(F32)
    trailing = jnp.where(docs == last, 1.0, 0.0).astype(F32)
    return living, trailing


def running_sum(gates):
    rows = gates.shape[0]
    lower = lax.broadcasted_iota(jnp.int32, (rows, rows), 0) >= lax.broadcasted_iota(
        jnp.int32, (rows, rows), 1
    )
    return dot(jnp.where(lower, 1.0, 0.0).astype(BF16), gates, NN)


def states_kernel(lens, q, k, v, gates, cot, weight, grad_o, fwd_o, bwd_o, decay_o):
    tokens = q.shape[0]
    bounds = bounds_of(lens)
    first = lax.axis_index("ctx") * tokens
    grad = dot(cot[...], weight[...], NT)
    grad_o[...] = grad
    cumulative = running_sum(gates[...])
    end = cumulative[tokens - 1 :, :]
    living, trailing = alive_and_trailing(bounds, first, tokens, KEY)
    tail = k[...].astype(F32) * jnp.exp(end - cumulative) * trailing
    alive = q[...].astype(F32) * SCALE * jnp.exp(cumulative) * living
    fwd_o[...] = product(whole(v[...]), split(tail), TN)
    bwd_o[...] = product(split(grad), split(alive), TN)
    decay_o[...] = (jnp.exp(end) * living[tokens - 1 :, :])[None]


def main_kernel(n, peers, pieces, norm, picks, *refs):
    if picks:
        refs = refs[:9] + refs[-2:] + refs[9:-2]
        cot = refs[11]
        refs = refs[:11] + refs[12:]
    (
        lens, q, k, v, gates, grad, fwd, bwd, decay, cot_own, cot_send,
        q_o, k_o, v_o, out,
        f_send, b_send, f_recv, b_recv, cum_s, attn_l, dq_l, dk_l, dv_l, fwd_c, bwd_c,
        cot_in, attn, attn_in, part, line_in,
        chain_sems, cot_sems, attn_send, attn_recv, line_send, line_recv,
    ) = refs
    me, dp, mp = lax.axis_index("ctx"), lax.axis_index("dp"), lax.axis_index("mp")
    tokens = q.shape[0]
    heads = decay.shape[0]
    blocks = tokens // SPAN
    cores = lax.axis_size("mp")
    right, left = lax.rem(me + 1, n), lax.rem(me + n - 1, n)
    others = [lax.rem(dp + s, peers) for s in range(1, peers)]
    mates = [lax.rem(mp + s, cores) for s in range(1, cores)]

    barrier = pltpu.get_barrier_semaphore()
    for other in others:
        pl.semaphore_signal(barrier, inc=1, device_id={"dp": other}, device_id_type=MESH)
    for near in (left, right):
        pl.semaphore_signal(barrier, inc=1, device_id={"ctx": near}, device_id_type=MESH)
    for mate in mates:
        pl.semaphore_signal(barrier, inc=1, device_id={"mp": mate}, device_id_type=MESH)
    pl.semaphore_wait(barrier, len(others) + 2 + len(mates))

    share = tokens // cores

    def remote(src, dst, send_sem, recv_sem, to):
        return pltpu.make_async_remote_copy(
            src_ref=src, dst_ref=dst, send_sem=send_sem, recv_sem=recv_sem,
            device_id=to, device_id_type=MESH,
        )

    def cot_copy(p):
        rows = pl.ds(pl.multiple_of(mp * share, share), share)
        return remote(
            cot_send.at[p, rows], cot_in.at[p, rows], cot_sems.at[0, p, 0], cot_sems.at[1, p, 0],
            {"dp": others[p]},
        )

    def mate_copy(p, m):
        rows = pl.ds(pl.multiple_of(mp * share, share), share)
        return remote(
            cot_in.at[p, rows], cot_in.at[p, rows], cot_sems.at[0, p, m + 1],
            cot_sems.at[1, p, m + 1], {"mp": mates[m]},
        )

    def pick_columns():
        width = cot_own.shape[1] // n
        for c in range(n):
            to = slice(c * width, (c + 1) * width)
            for s in range(peers):
                start = (c * peers + lax.rem(dp + s, peers)) * width
                mine = cot[:, pl.ds(pl.multiple_of(start, width), width)]
                if s == 0:
                    cot_own[:, to] = mine
                else:
                    cot_send[s - 1, :, to] = mine.astype(F32)

    rows_each = fwd.shape[0] // pieces
    per_head = pieces // heads
    has_left, has_right = me > 0, me < n - 1

    def chain_copy(c, send, recv, base, to):
        at = pl.ds(pl.multiple_of(c * rows_each, rows_each), rows_each)
        return remote(
            send.at[at], recv.at[at], chain_sems.at[base, c], chain_sems.at[base + 1, c], {"ctx": to}
        )

    def chain_piece(c, own, send, recv, base, has_source, has_target, to):
        at = pl.ds(pl.multiple_of(c * rows_each, rows_each), rows_each)

        @pl.when(has_source)
        def _():
            chain_copy(c, send, recv, base, to).wait_recv()

        @pl.when(jnp.logical_not(has_source))
        def _():
            recv[at, :] = jnp.zeros((rows_each, KEY), F32)

        @pl.when(has_target)
        def _():
            send[at, :] = decay[c // per_head] * recv[at, :] + own[at, :]
            chain_copy(c, send, recv, base, to).start()

    def slot(s, carry):
        up = s - SKEW * me
        down = s - SKEW * (n - 1 - me)

        @pl.when((up >= 0) & (up < pieces))
        def _():
            chain_piece(up, fwd, f_send, f_recv, 0, has_left, has_right, right)

        @pl.when((down >= 0) & (down < pieces))
        def _():
            chain_piece(down, bwd, b_send, b_recv, 2, has_right, has_left, left)

        return carry

    bounds = bounds_of(lens)
    device_first = me * tokens

    def of_head(h, n_block):
        at = slice(n_block * SPAN, (n_block + 1) * SPAN)
        return at, slice(h * KEY, (h + 1) * KEY), slice(h * VAL, (h + 1) * VAL)

    def inner(h, n_block):
        at, hk, hv = of_head(h, n_block)
        first = device_first + n_block * SPAN
        cumulative = running_sum(gates[at, hk])
        cum_s[at, hk] = cumulative
        growth = jnp.exp(cumulative)
        shrink = jnp.exp(-cumulative)
        end = cumulative[SPAN - 1 :, :]
        living, trailing = alive_and_trailing(bounds, first, SPAN, KEY)
        rows = lax.broadcasted_iota(jnp.int32, (SPAN, SPAN), 0)
        columns = lax.broadcasted_iota(jnp.int32, (SPAN, SPAN), 1)
        same = doc_array(bounds, first, (SPAN, SPAN), 0) == doc_array(bounds, first, (SPAN, SPAN), 1)
        mask = jnp.where((rows >= columns) & same, 1.0, 0.0).astype(F32)
        value = whole(v[at, hv])
        key = k[at, hk].astype(F32)
        grown = q[at, hk].astype(F32) * SCALE * growth
        grown_p, shrunk_p, grad_p = split(grown), split(key * shrink), split(grad[at, hv])
        scores = split(product(grown_p, shrunk_p, NT) * mask)
        mixing = split(product(grad_p, value, NT) * mask)
        attn_l[at, hv] = product(scores, value, NN)
        dq_l[at, hk] = product(mixing, shrunk_p, NN)
        dk_l[at, hk] = shrink * product(mixing, grown_p, TN)
        dv_l[at, hv] = product(scores, grad_p, TN)
        if n_block < blocks - 1:
            tail = split(key * jnp.exp(end - cumulative) * trailing)
            fwd_c[h, n_block] = product(value, tail, TN)
        if n_block > 0:
            bwd_c[h, n_block - 1] = product(grad_p, split(grown * living), TN)

    def attn_copy(p, j):
        return remote(
            attn.at[j], attn_in.at[p, j], attn_send.at[p, j], attn_recv.at[p, j], {"dp": others[p]}
        )

    parts_of_head = VAL // PIECE

    def forward(h):
        state = f_recv[h * VAL : (h + 1) * VAL, :]
        for b in range(blocks):
            at, hk, hv = of_head(h, b)
            cumulative = cum_s[at, hk]
            growth = jnp.exp(cumulative)
            living, _ = alive_and_trailing(bounds, device_first + b * SPAN, SPAN, KEY)
            alive = split(q[at, hk].astype(F32) * SCALE * growth * living)
            state_p = split(state)
            total = attn_l[at, hv] + product(alive, state_p, NT)
            total = total.astype(BF16).astype(F32)
            for p in range(parts_of_head):
                attn[h * parts_of_head + p, at, :] = total[:, p * PIECE : (p + 1) * PIECE]
            dq = dq_l[at, hk] + living * product(split(grad[at, hv]), state_p, NN)
            q_o[at, hk] = (growth * dq * SCALE).astype(BF16)
            if b < blocks - 1:
                keep = growth[SPAN - 1 :, :] * living[SPAN - 1 :, :]
                state = keep * state + fwd_c[h, b]

    def backward(h):
        state = b_recv[h * VAL : (h + 1) * VAL, :]
        for b in reversed(range(blocks)):
            at, hk, hv = of_head(h, b)
            cumulative = cum_s[at, hk]
            end = cumulative[SPAN - 1 :, :]
            living, trailing = alive_and_trailing(bounds, device_first + b * SPAN, SPAN, KEY)
            from_end = jnp.exp(end - cumulative) * trailing
            tail = split(k[at, hk].astype(F32) * from_end)
            state_p = split(state)
            dk = dk_l[at, hk] + from_end * product(whole(v[at, hv]), state_p, NN)
            k_o[at, hk] = dk.astype(BF16)
            v_o[at, hv] = (dv_l[at, hv] + product(tail, state_p, NT)).astype(BF16)
            if b > 0:
                keep = jnp.exp(end) * living[SPAN - 1 :, :]
                state = keep * state + bwd_c[h, b - 1]

    columns = out.shape[1]
    parts = attn.shape[0]

    def line_copy(j, c, up):
        place = c if up else jnp.where(me - 1 == c, n, c)
        return remote(
            part.at[j, c], line_in.at[j, place], line_send.at[j, c], line_recv.at[j, place],
            {"ctx": right if up else left},
        )

    def arrival(j, place, up):
        return remote(
            part.at[j, 0], line_in.at[j, place], line_send.at[j, 0], line_recv.at[j, place],
            {"ctx": right if up else left},
        )

    def multiply(j):
        total = dot(attn[j].astype(BF16), cot_own[...], TN)
        for p in range(peers - 1):
            attn_copy(p, j).wait_recv()
            total = total + dot(attn_in[p, j].astype(BF16), cot_in[p].astype(BF16), TN)
        for c in range(n):
            part[j, c] = total[:, c * columns : (c + 1) * columns]

    def sent(j, c):
        return remote(
            part.at[j, c], line_in.at[j, c], line_send.at[j, c], line_recv.at[j, c], {"ctx": right}
        )

    def send_off(j):
        for c in reversed(range(1, n)):

            @pl.when(me == 0)
            def _():
                line_copy(j, c, True).start()

        for c in range(n - 1):

            @pl.when(me == n - 1)
            def _():
                line_copy(j, c, False).start()

    def add_and_send(j, c, up):
        arrival(j, c, up).wait_recv()
        part[j, c] = part[j, c] + line_in[j, c]
        line_copy(j, c, up).start()

    def pass_on(j):
        for c in reversed(range(1, n)):

            @pl.when((me < c) & has_left)
            def _():
                add_and_send(j, c, True)

        for c in range(n - 1):

            @pl.when((me > c) & has_right)
            def _():
                add_and_send(j, c, False)

    def settle(j):
        at = pl.ds(j * PIECE, PIECE)
        out[at, :] = part[j, me] * norm

        @pl.when(has_left)
        def _():
            arrival(j, me, True).wait_recv()
            out[at, :] = out[at, :] + line_in[j, me] * norm

        @pl.when(has_right)
        def _():
            arrival(j, n, False).wait_recv()
            out[at, :] = out[at, :] + line_in[j, n] * norm

    def send_head(h):
        forward(h)
        for j in range(h * parts_of_head, (h + 1) * parts_of_head):
            for p in range(peers - 1):
                attn_copy(p, j).start()

    def slots_with(first, last, units):
        done = first
        for i, unit in enumerate(units):
            until = first + (i + 1) * (last - first) // len(units)
            lax.fori_loop(done, until, slot, 0)
            done = until
            inner(*unit)
        lax.fori_loop(done, last, slot, 0)

    begun, through = 3, per_head + SKEW * (n - 1)
    lax.fori_loop(0, begun, slot, 0)
    if picks:
        pick_columns()
    for p in range(peers - 1):
        cot_copy(p).start()
    slots_with(begun, through, [(0, b) for b in range(blocks)])
    send_head(0)
    later = [(h, b) for h in range(1, heads) for b in range(blocks)]
    slots_with(through, pieces + SKEW * (n - 1), later[: blocks // 2])
    for p in range(peers - 1):
        cot_copy(p).wait_recv()
        for m in range(cores - 1):
            mate_copy(p, m).start()
    for p in range(peers - 1):
        for m in range(cores - 1):
            mate_copy(p, m).wait_recv()
    multiply(0)
    send_off(0)
    for unit in later[blocks // 2 :]:
        inner(*unit)
    for h in range(1, heads):
        send_head(h)
    pass_on(0)
    for j in range(1, parts):
        multiply(j)
        send_off(j)
        pass_on(j)
        if j <= heads:
            backward(j - 1)
    for j in range(parts):
        settle(j)

    def finish(c, carry):
        @pl.when(has_right)
        def _():
            chain_copy(c, f_send, f_recv, 0, right).wait_send()

        @pl.when(has_left)
        def _():
            chain_copy(c, b_send, b_recv, 2, left).wait_send()

        return carry

    lax.fori_loop(0, pieces, finish, 0)
    for p in range(peers - 1):
        cot_copy(p).wait_send()
        for m in range(cores - 1):
            mate_copy(p, m).wait_send()
    for j in range(parts):
        for p in range(peers - 1):
            attn_copy(p, j).wait_send()
        for c in range(n):

            @pl.when(me != c)
            def _():
                sent(j, c).wait_send()


def params(**more):
    return pltpu.CompilerParams(vmem_limit_bytes=VMEM_BYTES, **more)


def per_device(queries, key_vectors, value_vectors, log_gates, doc_lengths, cotangent, out_weight):
    q, k, v, gates, cot = (x[0] for x in (queries, key_vectors, value_vectors, log_gates, cotangent))
    tokens, width = cot.shape
    heads = out_weight.shape[0] // VAL
    n, peers = lax.axis_size("ctx"), lax.axis_size("dp")
    dp = lax.axis_index("dp")
    columns = width // (n * peers)
    smem = pl.BlockSpec(memory_space=pltpu.SMEM)

    in_kernel = columns % 128 == 0
    spread = n * columns

    def head_block(rows, cols):
        return pl.BlockSpec((rows, cols), lambda h: (0, h))

    def head_rows(rows, cols):
        return pl.BlockSpec((rows, cols), lambda h: (h, 0))

    grad, fwd, bwd, decay = pl.pallas_call(
        states_kernel,
        grid=(heads,),
        in_specs=[
            smem,
            head_block(tokens, KEY),
            head_block(tokens, KEY),
            head_block(tokens, VAL),
            head_block(tokens, KEY),
            pl.BlockSpec((tokens, width), lambda h: (0, 0)),
            head_rows(VAL, width),
        ],
        out_specs=[
            head_block(tokens, VAL),
            head_rows(VAL, KEY),
            head_rows(VAL, KEY),
            pl.BlockSpec((1, 1, KEY), lambda h: (h, 0, 0)),
        ],
        out_shape=[
            jax.ShapeDtypeStruct((tokens, heads * VAL), F32),
            jax.ShapeDtypeStruct((heads * VAL, KEY), F32),
            jax.ShapeDtypeStruct((heads * VAL, KEY), F32),
            jax.ShapeDtypeStruct((heads, 1, KEY), F32),
        ],
        compiler_params=params(),
        cost_estimate=pl.CostEstimate(flops=6 * 10**9, bytes_accessed=14 << 20, transcendentals=0),
        name="states",
    )(doc_lengths, q, k, v, gates, cot, out_weight)

    if in_kernel:
        cots = [cot]
    else:
        parted = cot.reshape(tokens, n, peers, columns)
        shares = [
            lax.dynamic_index_in_dim(parted, lax.rem(dp + s, peers), axis=2, keepdims=False).reshape(
                tokens, spread
            )
            for s in range(peers)
        ]
        cots = [shares[0], jnp.stack(shares[1:]).astype(F32)]

    pieces = 8 * heads
    vmem = pl.BlockSpec(memory_space=pltpu.VMEM)
    states = (heads * VAL, KEY)
    keys, values = (tokens, heads * KEY), (tokens, heads * VAL)
    parts = heads * VAL // PIECE
    blocks = tokens // SPAN
    cores = lax.axis_size("mp")
    dma = pltpu.SemaphoreType.DMA
    norm = 1.0 / math.sqrt(peers * n * tokens)
    scratch = (
        [states] * 4
        + [keys, values, keys, keys, values]
        + [(heads, blocks - 1, VAL, KEY)] * 2
        + [
            (peers - 1, tokens, spread),
            (parts, tokens, PIECE),
            (peers - 1, parts, tokens, PIECE),
            (parts, n, PIECE, columns),
            (parts, n + 1, PIECE, columns),
        ]
    )
    query_grad, key_grad, value_grad, weight_grad = pl.pallas_call(
        functools.partial(main_kernel, n, peers, pieces, norm, in_kernel),
        in_specs=[smem] + [vmem] * (8 + len(cots)),
        out_specs=[vmem] * 4,
        out_shape=[
            jax.ShapeDtypeStruct(keys, BF16),
            jax.ShapeDtypeStruct(keys, BF16),
            jax.ShapeDtypeStruct(values, BF16),
            jax.ShapeDtypeStruct((heads * VAL, columns), F32),
        ],
        scratch_shapes=[pltpu.VMEM(shape, F32) for shape in scratch]
        + [
            dma((4, pieces)),
            dma((2, peers - 1, cores)),
            dma((peers - 1, parts)),
            dma((peers - 1, parts)),
            dma((parts, n)),
            dma((parts, n + 1)),
        ]
        + [pltpu.VMEM((tokens, spread), BF16), pltpu.VMEM((peers - 1, tokens, spread), F32)]
        * in_kernel,
        compiler_params=params(collective_id=0, has_side_effects=True),
        cost_estimate=pl.CostEstimate(flops=10**10, bytes_accessed=64 << 20, transcendentals=0),
        name="main",
    )(doc_lengths, q, k, v, gates, grad, fwd, bwd, decay, *cots)
    return (query_grad[None], key_grad[None], value_grad[None], weight_grad)


def solution(mesh):
    batch = ("groups", "dp")
    return jax.shard_map(
        per_device,
        mesh=mesh,
        in_specs=(
            P(batch, "ctx", "mp"),
            P(batch, "ctx", "mp"),
            P(batch, "ctx", "mp"),
            P(batch, "ctx", "mp"),
            P(batch, None),
            P(batch, "ctx", None),
            P("mp", None),
        ),
        out_specs=(
            P(batch, "ctx", "mp"),
            P(batch, "ctx", "mp"),
            P(batch, "ctx", "mp"),
            P(("groups", "mp"), ("ctx", "dp")),
        ),
        check_vma=False,
    )
```
